512 devices in a mesh: head: 8 (over y), blk: 64 (over z, x, core).
Axes of the slice: x: 4, y: 8, z: 8, core: 2. Of those that a mesh axis runs over, the one named last changes fastest.
Arguments:
- residual: bfloat16 [12288, 2048], P('blk'), may hold values from -100 to 100
- lengths: int32 [64, 6], P('blk'), may hold values from 1 to 96, 192 in all within a row
- token_adapter_index: int32 [12288, 1], P('blk'), may hold values from 0 to 63; in each aligned block of 192 rows (0 to 191, 192 to 383, ...) at most 6 rows name the same one
- attention_norm_gain: float32 [2048], replicated, may hold values from 0.1 to 1.9
- query_key_weight: bfloat16 [2048, 4096], P('blk', 'head'), may hold values from -8 to 8
- value_weight: bfloat16 [2048, 2048], P('blk', 'head'), may hold values from -0.125 to 0.125
- head_second_weight: float32 [8], P('head'), may hold values from 0.2 to 0.8
- output_weight: bfloat16 [2048, 2048], P('blk', 'head'), may hold values from -0.125 to 0.125
- adapter_down_maps: bfloat16 [64, 2048, 16], P('blk', 'head'), may hold values from -0.125 to 0.125
- adapter_up_maps: bfloat16 [64, 16, 2048], P('blk'), may hold values from -1.5 to 1.5
- feedforward_norm_gain: float32 [2048], replicated, may hold values from 0.1 to 1.9
- gate_weight: bfloat16 [2048, 5632], P('blk', 'head'), may hold values from -0.125 to 0.125
- up_weight: bfloat16 [2048, 5632], P('blk', 'head'), may hold values from -0.125 to 0.125
- down_weight: bfloat16 [2048, 5632], P('blk', 'head'), may hold values from -0.078125 to 0.078125
Outputs:
- layer_out: bfloat16 [12288, 2048], P('blk', 'head')
The draws below stay inside these ranges and needn't reach their ends.
Inputs may be any that keep to these rules, and one draw needn't show every extreme that they name: `lengths`: each row sums to 192, and its largest entry is 96. `token_adapter_index`: among the 192 tokens of one block no adapter is named more than 6 times, a bound that some block reaches.
All inputs are finite; a program needn't handle non-finite values.
Results may differ from the reference program's by a relative error of at most 0.011.
Values may be sent and summed in bfloat16 or wider, within the bound.
No kernel may reach another device: no remote copies, remote signals or barrier semaphores. Data moves between devices by JAX's collectives and lax.ppermute only.
A program may use at most 64 MiB of HBM per device.

```python
import math
import jax
import jax.numpy as jnp
import numpy as np
from jax import lax

MODEL_WIDTH = 2048
FF = 5632
HD = 128
VALUE_WIDTH = 256
ADAPTER_RANK = 16
SEQ_DEV = 6
TOK_DEV = 192
HEAD_COUNT = 8
ADAPTER_COUNT = 64
BLOCKS = 64
TOKENS = 12288
CAP = 6
MOST_LEN = 96


def draw_residual(key, part):
    key_rows, key_cols, key_main = jax.random.split(key, 3)
    position = jnp.arange(MODEL_WIDTH, dtype=jnp.float32) / MODEL_WIDTH
    column_scale = (10.0 ** (position - 0.5))[None, :] * 2.0 ** jax.random.uniform(key_cols, (1, MODEL_WIDTH), jnp.float32, -0.5, 0.5)
    row_scale = 10.0 ** (jax.random.uniform(key_rows, (TOKENS, 1), jnp.float32) - 0.5)
    noise = jnp.clip(jax.random.normal(key_main, (TOKENS, MODEL_WIDTH), jnp.float32), -4.0, 4.0)
    return (noise * row_scale * column_scale).astype(jnp.bfloat16)


def draw_query_key_weight(key, part):
    base = jnp.clip(jax.random.normal(key, (MODEL_WIDTH, HEAD_COUNT, 4, HD), jnp.float32), -6.0, 6.0) / math.sqrt(MODEL_WIDTH)
    return base.reshape(MODEL_WIDTH, HEAD_COUNT * 4 * HD).astype(jnp.bfloat16)


def block_levels(stream_key, shape, pieces, least, largest):
    factor_of, own = 1.0, jax.random.fold_in(stream_key, 6)
    for dim, parts in pieces:
        draws = jnp.exp(jax.random.uniform(jax.random.fold_in(own, dim), (parts,), jnp.float32, least / len(pieces), largest / len(pieces)))
        factor_of = factor_of * jnp.repeat(draws, shape[dim] // parts).reshape([-1 if axis == dim else 1 for axis in range(len(shape))])
    return factor_of


def split_up(amount, total, most, skew):
    weights = [(1 << 20) // math.isqrt(rank ** skew) + 1 for rank in range(2, amount + 1)]
    surplus, holding = total - most - (amount - 1), [1] * (amount - 1)
    while surplus > 0:
        movable = [i for i in range(amount - 1) if holding[i] < most]
        mass, budget = sum([weights[i] for i in movable]), surplus
        for i in movable:
            addition = min(most - holding[i], max(1, budget * weights[i] // mass), surplus)
            holding[i] = holding[i] + addition
            surplus = surplus - addition
    return np.array([most] + holding)


def ragged(own_key, count, total, bound, slope):
    if count == 2:
        one = jax.random.randint(own_key, (), max(1, total - bound), min(bound, total - 1) + 1)
        return jnp.stack([one, total - one])
    sizes = jnp.asarray(split_up(count, total, bound, slope), jnp.int32)
    couples = (count - 1) // 2
    giver, taker = sizes[1:1 + 2 * couples:2], sizes[2:2 + 2 * couples:2]
    room = jnp.minimum(giver - 1, bound - taker)
    moved = jax.random.randint(jax.random.fold_in(own_key, 1), (couples,), 0, 1 << 20) % (room + 1)
    sizes = sizes.at[1:1 + 2 * couples:2].set(giver - moved).at[2:2 + 2 * couples:2].set(taker + moved)
    return sizes[jax.random.permutation(jax.random.fold_in(own_key, 2), count)]


def shared_out(stream_key, own, number, rows, number_of, top, limit, lean):
    sequence = jax.random.permutation(stream_key, number_of)
    packed, common = shares(number_of, rows * top, limit, lean, True), shares(number_of, rows * top, limit, lean, False)
    places = jnp.arange(number_of)

    def named(sizes, offset_by):
        used = int((sizes > 0).sum())
        fixed = max(1, used // 4)
        moved = fixed + (places - fixed + offset_by * (used - fixed)) % max(1, number_of - fixed)
        return jnp.zeros((number_of,), jnp.int32).at[sequence[jnp.where(places < fixed, places, moved)]].set(jnp.asarray(sizes, jnp.int32))

    sizes = jnp.where(number % 4 == 0, named(packed, number // 4), named(common, number - number // 4 - 1))
    mixed = jax.random.permutation(jax.random.fold_in(own, 3), number_of)
    giver, receiver = mixed[0:number_of // 2 * 2:2], mixed[1:number_of // 2 * 2:2]
    room = jnp.minimum(sizes[giver] - 1, limit - sizes[receiver]) // 2
    room = jnp.where((giver == sequence[0]) | (receiver == sequence[0]) | (sizes[receiver] == 0), 0, jnp.maximum(room, 0))
    moved = jax.random.randint(jax.random.fold_in(own, 4), (number_of // 2,), 0, 1 << 20) % (room + 1)
    sizes = sizes.at[giver].add(-moved).at[receiver].add(moved)
    members = jnp.searchsorted(jnp.cumsum(sizes), jnp.arange(rows * top), side="right").astype(jnp.int32)
    table = members.reshape(top, rows).T
    table = table[jax.random.permutation(jax.random.fold_in(own, 1), rows)]
    offset_by = jax.random.randint(jax.random.fold_in(own, 2), (rows, 1), 0, top)
    return jnp.take_along_axis(table, (jnp.arange(top)[None, :] + offset_by) % top, axis=1)


def shares(amount, total, bound, skew, full):
    loads = [(1 << 20) // math.isqrt(rank ** skew) + 1 for rank in range(1, amount + 1)]
    largest = bound if full else min(bound, max(-(-total // amount), total * loads[0] // sum(loads)))
    least = 1 if total - largest >= amount - 1 else 0
    given, rest = [largest] + [least] * (amount - 1), total - largest - least * (amount - 1)
    while rest > 0:
        free = [i for i in range(1, amount) if given[i] < largest] or [i for i in range(1, amount) if given[i] < bound]
        pool, remaining = sum([loads[i] for i in free]), rest
        for i in free:
            addition = min(bound - given[i], max(1, remaining * loads[i] // pool), rest)
            given[i] = given[i] + addition
            rest = rest - addition
    return np.array(given)


def centred(key, dims, width, bound, shards=(), kind=jnp.bfloat16):
    array = jax.random.normal(key, dims, jnp.float32) * width
    if len(shards) > 0:
        array = block_levels(key, dims, shards, -0.22, 0.18) * array
    return jnp.clip(array, min=-bound, max=bound).astype(kind)


def setup_inputs(seed: int = 0) -> dict:
    key_list = jax.random.split(jax.random.key(seed), 15)
    residual = draw_residual(jax.random.fold_in(key_list[14], 71), 0)
    lengths = jax.vmap(lambda own: ragged(own, SEQ_DEV, TOK_DEV, MOST_LEN, 2))(jax.random.split(key_list[1], BLOCKS)).reshape((BLOCKS, SEQ_DEV)).astype(jnp.int32)
    token_adapter_index_keys = jax.random.split(jax.random.fold_in(key_list[2], 1), TOKENS // TOK_DEV)
    token_adapter_index_turns = jax.random.permutation(jax.random.fold_in(key_list[2], 3), TOKENS // TOK_DEV)
    token_adapter_index = jax.vmap(lambda own, number: shared_out(jax.random.fold_in(key_list[2], 2), own, number, TOK_DEV, ADAPTER_COUNT, 1, CAP, 2))(token_adapter_index_keys, token_adapter_index_turns).reshape((TOKENS, 1))
    attention_norm_gain = jnp.clip(1.0 + 0.18 * jax.random.normal(key_list[3], (MODEL_WIDTH,), jnp.float32), 0.1, 1.9)
    query_key_weight = draw_query_key_weight(jax.random.fold_in(key_list[14], 71), 0)
    value_weight = centred(key_list[5], (MODEL_WIDTH, HEAD_COUNT * VALUE_WIDTH), MODEL_WIDTH ** -0.5, 0.125, ((0, 64), (1, 8)))
    head_second_weight = jnp.clip(0.2 + 0.6 * jax.random.uniform(key_list[6], (HEAD_COUNT,), jnp.float32) ** block_levels(key_list[6], (HEAD_COUNT,), ((0, 8),), -0.2, 0.2), 0.2, 0.8)
    output_weight = centred(key_list[7], (MODEL_WIDTH, HEAD_COUNT * VALUE_WIDTH), (HEAD_COUNT * VALUE_WIDTH) ** -0.5, 0.125, ((0, 64), (1, 8)))
    adapter_down_maps = centred(key_list[8], (ADAPTER_COUNT, HEAD_COUNT * VALUE_WIDTH, ADAPTER_RANK), (HEAD_COUNT * VALUE_WIDTH) ** -0.5, 0.125, ((0, 64), (1, 8)))
    adapter_up_maps = centred(key_list[9], (ADAPTER_COUNT, ADAPTER_RANK, MODEL_WIDTH), ADAPTER_RANK ** -0.5, 1.5, ((0, 64),))
    feedforward_norm_gain = jnp.clip(1.0 + 0.18 * jax.random.normal(key_list[10], (MODEL_WIDTH,), jnp.float32), 0.1, 1.9)
    gate_weight = centred(key_list[11], (MODEL_WIDTH, FF), MODEL_WIDTH ** -0.5, 0.125, ((0, 64), (1, 8)))
    up_weight = centred(key_list[12], (MODEL_WIDTH, FF), MODEL_WIDTH ** -0.5, 0.125, ((0, 64), (1, 8)))
    down_weight = centred(key_list[13], (MODEL_WIDTH, FF), FF ** -0.5, 0.078125, ((0, 64), (1, 8)))
    return {"residual": residual, "lengths": lengths, "token_adapter_index": token_adapter_index, "attention_norm_gain": attention_norm_gain, "query_key_weight": query_key_weight, "value_weight": value_weight, "head_second_weight": head_second_weight, "output_weight": output_weight, "adapter_down_maps": adapter_down_maps, "adapter_up_maps": adapter_up_maps, "feedforward_norm_gain": feedforward_norm_gain, "gate_weight": gate_weight, "up_weight": up_weight, "down_weight": down_weight}


adapter_scaling = 2.0
head_shrink = 0.8
neg_large = -1e+30

def rms_scale(values, epsilon):
    return values * lax.rsqrt(lax.optimization_barrier(jnp.mean(values * values, axis=-1, keepdims=True)) + epsilon)

def masked_softmax(scores, allowed):
    scores = jnp.where(allowed, scores, neg_large)
    row_peak = lax.optimization_barrier(jnp.max(scores, axis=-1, keepdims=True))
    raised = jnp.where(allowed, jnp.exp(scores - row_peak), 0.0)
    return raised / lax.optimization_barrier(jnp.sum(raised, axis=-1, keepdims=True))

def request_mask(lengths_row, length_total):
    ends_at = jnp.cumsum(lengths_row.astype(jnp.int32))
    position = jnp.arange(length_total, dtype=jnp.int32)
    request = lax.optimization_barrier(jnp.sum((position[:, None] >= ends_at[None, :]).astype(jnp.int32), axis=1))
    return (request[:, None] == request[None, :]) & (position[None, :] <= position[:, None])

def diff_head(qk_head, value_head, allowed, lambda_value):
    score_scale = 1.0 / qk_head.shape[-1] ** 0.5
    first_scores = jnp.dot(qk_head[:, 0], qk_head[:, 2].T, precision=lax.Precision.HIGHEST) * score_scale
    second_scores = jnp.dot(qk_head[:, 1], qk_head[:, 3].T, precision=lax.Precision.HIGHEST) * score_scale
    mixed = (masked_softmax(first_scores, allowed) - lambda_value * masked_softmax(second_scores, allowed)).astype(jnp.bfloat16)
    attended = jnp.dot(mixed, value_head, preferred_element_type=jnp.float32)
    return (rms_scale(attended, 1e-05) * head_shrink).astype(jnp.bfloat16)

def reference(residual, lengths, token_adapter_index, attention_norm_gain, query_key_weight, value_weight, head_second_weight, output_weight, adapter_down_maps, adapter_up_maps, feedforward_norm_gain, gate_weight, up_weight, down_weight):

    def one_block(operands):
        block_rows, lengths_row, adapter_table = operands
        inputs = block_rows.astype(jnp.float32)
        normed = (rms_scale(inputs, 1e-06) * attention_norm_gain).astype(jnp.bfloat16)
        qk_all = jnp.dot(normed, query_key_weight, preferred_element_type=jnp.float32).reshape(TOK_DEV, HEAD_COUNT, 4, HD)
        value_all = jnp.dot(normed, value_weight, preferred_element_type=jnp.float32).astype(jnp.bfloat16).reshape(TOK_DEV, HEAD_COUNT, VALUE_WIDTH)
        allowed = request_mask(lengths_row, TOK_DEV)
        share_sum = jnp.zeros((TOK_DEV, MODEL_WIDTH), jnp.float32)
        head_list = []
        for head_idx in range(HEAD_COUNT):
            begin_col = head_idx * VALUE_WIDTH
            head_out = diff_head(qk_all[:, head_idx], value_all[:, head_idx], allowed, head_second_weight[head_idx])
            head_list.append(head_out)
            head_share = jnp.dot(head_out, output_weight[:, begin_col:begin_col + VALUE_WIDTH].T, preferred_element_type=jnp.float32).astype(jnp.bfloat16)
            head_share = lax.optimization_barrier(head_share)
            share_sum = share_sum + head_share.astype(jnp.float32)
        all_heads = jnp.concatenate(head_list, axis=1).astype(jnp.float32)
        selected_down_maps = adapter_down_maps[adapter_table].astype(jnp.float32)
        selected_up_maps = adapter_up_maps[adapter_table].astype(jnp.float32)
        reduced_rank_state = jnp.einsum('tk,tkr->tr', all_heads, selected_down_maps, precision=lax.Precision.HIGHEST).astype(jnp.bfloat16)
        adapter_delta = (adapter_scaling * jnp.einsum('tr,trd->td', reduced_rank_state.astype(jnp.float32), selected_up_maps, precision=lax.Precision.HIGHEST)).astype(jnp.bfloat16)
        mid_state = inputs + share_sum + adapter_delta.astype(jnp.float32)
        mid_round = mid_state.astype(jnp.bfloat16)
        ffn_in = (rms_scale(mid_round.astype(jnp.float32), 1e-06) * feedforward_norm_gain).astype(jnp.bfloat16)
        gate_act = jnp.dot(ffn_in, gate_weight, preferred_element_type=jnp.float32)
        upward = jnp.dot(ffn_in, up_weight, preferred_element_type=jnp.float32)
        hidden_units = (jax.nn.silu(gate_act) * upward).astype(jnp.bfloat16)
        unit_count = FF // HEAD_COUNT
        ffn_total = jnp.zeros((TOK_DEV, MODEL_WIDTH), jnp.float32)
        for group_idx in range(HEAD_COUNT):
            begin_unit = group_idx * unit_count
            ffn_piece = jnp.dot(hidden_units[:, begin_unit:begin_unit + unit_count], down_weight[:, begin_unit:begin_unit + unit_count].T, preferred_element_type=jnp.float32).astype(jnp.bfloat16)
            ffn_piece = lax.optimization_barrier(ffn_piece)
            ffn_total = ffn_total + ffn_piece.astype(jnp.float32)
        return (mid_state + ffn_total).astype(jnp.bfloat16)
    blocks = (residual.reshape(BLOCKS, TOK_DEV, MODEL_WIDTH), lengths, token_adapter_index.reshape(BLOCKS, TOK_DEV))
    result = lax.map(one_block, blocks)
    return result.reshape(TOKENS, MODEL_WIDTH)
```

```python
import jax
import jax.numpy as jnp
from jax import lax
from jax.sharding import Mesh
from jax.sharding import PartitionSpec as P

HD = 128
RANK = 16

adapter_scaling = 2.0
head_shrink = 0.8
neg_large = -1e30

BLK = ("z", "x", "core")


def rms_scale(values, epsilon):
    return values * lax.rsqrt(jnp.mean(values * values, axis=-1, keepdims=True) + epsilon)


def masked_softmax(scores, allowed):
    scores = jnp.where(allowed, scores, neg_large)
    row_peak = jnp.max(scores, axis=-1, keepdims=True)
    raised = jnp.where(allowed, jnp.exp(scores - row_peak), 0.0)
    return raised / jnp.sum(raised, axis=-1, keepdims=True)


def request_mask(lengths_row, length_total):
    count = lengths_row.shape[0]
    order = jnp.arange(count, dtype=jnp.int32)
    ends_at = jnp.sum(jnp.where(order[None, :] <= order[:, None], lengths_row[None, :], 0), axis=1)
    position = jnp.arange(length_total, dtype=jnp.int32)
    request = jnp.sum((position[:, None] >= ends_at[None, :]).astype(jnp.int32), axis=1)
    return (request[:, None] == request[None, :]) & (position[None, :] <= position[:, None])


def diff_head(qk_head, value_head, allowed, lambda_value):
    score_scale = 1.0 / HD**0.5
    parts = [qk_head[:, i * HD : (i + 1) * HD] for i in range(4)]

    def scores(left, right):
        return (
            lax.dot_general(left, right, (((1,), (1,)), ((), ())), precision=lax.Precision.HIGHEST)
            * score_scale
        )

    mixed = (
        masked_softmax(scores(parts[0], parts[2]), allowed)
        - lambda_value * masked_softmax(scores(parts[1], parts[3]), allowed)
    ).astype(jnp.bfloat16)
    attended = jnp.dot(mixed, value_head, preferred_element_type=jnp.float32)
    return (rms_scale(attended, 1e-05) * head_shrink).astype(jnp.bfloat16)


def exchange(blocks, axis):
    return lax.all_to_all(blocks, axis, split_axis=0, concat_axis=0, tiled=True)


def spread(block, axis):
    return exchange(jnp.broadcast_to(block[None], (lax.axis_size(axis), *block.shape)), axis)


def sibling(block):
    return lax.ppermute(block, "core", [(0, 1), (1, 0)])


def fold_map(rank_rows):
    half = rank_rows.shape[1] // 2
    return jnp.concatenate([rank_rows[:, :half], rank_rows[:, half:]], axis=0)


def unfold_map(folded, owners):
    stacked = folded.reshape(owners, 2, RANK, folded.shape[1])
    return [stacked[:, i].reshape(owners * RANK, folded.shape[1]) for i in range(2)]


def per_device(
    residual,
    lengths,
    token_adapter_index,
    attention_norm_gain,
    query_key_weight,
    value_weight,
    head_second_weight,
    output_weight,
    adapter_down_maps,
    adapter_up_maps,
    feedforward_norm_gain,
    gate_weight,
    up_weight,
    down_weight,
):
    tokens, width = residual.shape
    groups = lax.axis_size("head")
    owners = lax.axis_size(BLK)
    own_width = width // groups
    own_begin = lax.axis_index("head") * own_width
    units = gate_weight.shape[1]
    qk_width = query_key_weight.shape[1]
    value_width = value_weight.shape[1]

    down_map = fold_map(adapter_down_maps[0].T)
    up_map = fold_map(lax.dynamic_slice_in_dim(adapter_up_maps[0], own_begin, own_width, 1))

    late = lax.all_gather(
        jnp.concatenate([gate_weight, up_weight, up_map, down_weight], axis=1),
        BLK,
        axis=0,
        tiled=True,
    )

    early = jnp.concatenate([query_key_weight, value_weight, output_weight, down_map], axis=1)
    early_width = early.shape[1]
    mine = spread(spread(early, "z"), "x")
    other = sibling(mine)
    first = lax.axis_index("core") == 0
    both = jnp.stack([jnp.where(first, mine, other), jnp.where(first, other, mine)], axis=2)
    both = both.transpose(1, 0, 2, 3, 4).reshape(width, early_width)
    qk_full = both[:, :qk_width]
    value_full = both[:, qk_width : qk_width + value_width]
    out_full = both[:, qk_width + value_width : qk_width + 2 * value_width]
    down_maps = unfold_map(both[:, qk_width + 2 * value_width :], owners)

    inputs = residual.astype(jnp.float32)
    normed = (rms_scale(inputs, 1e-06) * attention_norm_gain).astype(jnp.bfloat16)
    qk_head = jnp.dot(normed, qk_full, preferred_element_type=jnp.float32)
    value_head = jnp.dot(normed, value_full, preferred_element_type=jnp.float32).astype(jnp.bfloat16)
    allowed = request_mask(lengths[0], tokens)
    head_out = diff_head(qk_head, value_head, allowed, head_second_weight[0])

    coordinate = jnp.arange(owners * RANK, dtype=jnp.int32)
    chosen = coordinate[None, :] // RANK == token_adapter_index
    lift = (jnp.arange(RANK, dtype=jnp.int32)[:, None] == coordinate[None, :] % RANK)
    half = value_width // 2
    all_coordinates = sum(
        lax.dot_general(
            head_out[:, i * half : (i + 1) * half],
            down_maps[i],
            (((1,), (1,)), ((), ())),
            preferred_element_type=jnp.float32,
        )
        for i in range(2)
    )
    low_part = lax.dot_general(
        lift.astype(jnp.float32),
        jnp.where(chosen, all_coordinates, 0.0),
        (((1,), (1,)), ((), ())),
        precision=lax.Precision.HIGHEST,
    )
    low_high = lax.reduce_precision(low_part, 8, 7)
    low_rows = jnp.concatenate([low_high, low_part - low_high], axis=0).astype(jnp.bfloat16)
    low_rows = jnp.pad(low_rows, ((0, 0), (0, own_width - tokens)))

    share = lax.dot_general(
        head_out, out_full, (((1,), (1,)), ((), ())), preferred_element_type=jnp.float32
    ).astype(jnp.bfloat16)
    share = share.reshape(tokens, groups, own_width).transpose(1, 0, 2)
    sent = jnp.concatenate(
        [share, jnp.broadcast_to(low_rows[None], (groups, *low_rows.shape))], axis=1
    )
    total = jnp.sum(exchange(sent, "head").astype(jnp.float32), axis=0)
    low_rank = (total[tokens : tokens + RANK, :tokens] + total[tokens + RANK :, :tokens]).astype(
        jnp.bfloat16
    )
    lifted = lax.dot_general(
        low_rank,
        lift.astype(jnp.bfloat16),
        (((0,), (0,)), ((), ())),
        preferred_element_type=jnp.float32,
    )
    routed = jnp.where(chosen, lifted, 0.0).astype(jnp.bfloat16)
    up_maps = unfold_map(late[:, 2 * units : 2 * units + own_width // 2], owners)
    delta_own = (
        adapter_scaling
        * jnp.concatenate(
            [jnp.dot(routed, part, preferred_element_type=jnp.float32) for part in up_maps], axis=1
        )
    ).astype(jnp.bfloat16)
    own_mid = (
        lax.dynamic_slice_in_dim(inputs, own_begin, own_width, 1)
        + total[:tokens]
        + delta_own.astype(jnp.float32)
    )
    mid_full = spread(own_mid.astype(jnp.bfloat16), "head").transpose(1, 0, 2).reshape(tokens, width)
    ffn_in = (rms_scale(mid_full.astype(jnp.float32), 1e-06) * feedforward_norm_gain).astype(
        jnp.bfloat16
    )
    both_acts = jnp.dot(ffn_in, late[:, : 2 * units], preferred_element_type=jnp.float32)
    hidden_units = (jax.nn.silu(both_acts[:, :units]) * both_acts[:, units:]).astype(jnp.bfloat16)
    piece = lax.dot_general(
        hidden_units,
        late[:, 2 * units + own_width // 2 :],
        (((1,), (1,)), ((), ())),
        preferred_element_type=jnp.float32,
    ).astype(jnp.bfloat16)
    piece = piece.reshape(tokens, groups, own_width).transpose(1, 0, 2)
    return (own_mid + jnp.sum(exchange(piece, "head").astype(jnp.float32), axis=0)).astype(
        jnp.bfloat16
    )


def solution(mesh):
    fine = Mesh(mesh.devices.reshape(mesh.devices.shape[0], 8, 4, 2), ("head", *BLK))
    return jax.shard_map(
        per_device,
        mesh=fine,
        in_specs=(
            P(BLK, None),
            P(BLK, None),
            P(BLK, None),
            P(),
            P(BLK, "head"),
            P(BLK, "head"),
            P("head"),
            P(BLK, "head"),
            P(BLK, "head", None),
            P(BLK, None, None),
            P(),
            P(BLK, "head"),
            P(BLK, "head"),
            P(BLK, "head"),
        ),
        out_specs=P(BLK, "head"),
        check_vma=False,
    )
```

```python
import jax
import jax.numpy as jnp
from jax import lax
from jax.sharding import Mesh
from jax.sharding import PartitionSpec as P

HD = 128
RANK = 16

adapter_scaling = 2.0
head_shrink = 0.8
neg_large = -1e30

BLK = ("z", "x", "core")


def rms_scale(values, epsilon):
    return values * lax.rsqrt(jnp.mean(values * values, axis=-1, keepdims=True) + epsilon)


def masked_softmax(scores, allowed):
    scores = jnp.where(allowed, scores, neg_large)
    row_peak = jnp.max(scores, axis=-1, keepdims=True)
    raised = jnp.where(allowed, jnp.exp(scores - row_peak), 0.0)
    return raised / jnp.sum(raised, axis=-1, keepdims=True)


def request_mask(lengths_row, length_total):
    count = lengths_row.shape[0]
    order = jnp.arange(count, dtype=jnp.int32)
    ends_at = jnp.sum(jnp.where(order[None, :] <= order[:, None], lengths_row[None, :], 0), axis=1)
    position = jnp.arange(length_total, dtype=jnp.int32)
    request = jnp.sum((position[:, None] >= ends_at[None, :]).astype(jnp.int32), axis=1)
    return (request[:, None] == request[None, :]) & (position[None, :] <= position[:, None])


def diff_head(qk_head, value_head, allowed, lambda_value):
    score_scale = 1.0 / HD**0.5
    parts = [qk_head[:, i * HD : (i + 1) * HD] for i in range(4)]

    def scores(left, right):
        return (
            lax.dot_general(left, right, (((1,), (1,)), ((), ())), precision=lax.Precision.HIGHEST)
            * score_scale
        )

    mixed = (
        masked_softmax(scores(parts[0], parts[2]), allowed)
        - lambda_value * masked_softmax(scores(parts[1], parts[3]), allowed)
    ).astype(jnp.bfloat16)
    attended = jnp.dot(mixed, value_head, preferred_element_type=jnp.float32)
    return (rms_scale(attended, 1e-05) * head_shrink).astype(jnp.bfloat16)


def exchange(blocks, axis):
    return lax.all_to_all(blocks, axis, split_axis=0, concat_axis=0, tiled=True)


def spread(block, axis):
    return exchange(jnp.broadcast_to(block[None], (lax.axis_size(axis), *block.shape)), axis)


def sibling(block):
    return lax.ppermute(block, "core", [(0, 1), (1, 0)])


def fold_map(rank_rows):
    half = rank_rows.shape[1] // 2
    return jnp.concatenate([rank_rows[:, :half], rank_rows[:, half:]], axis=0)


def unfold_map(folded, owners):
    stacked = folded.reshape(owners, 2, RANK, folded.shape[1])
    return [stacked[:, i].reshape(owners * RANK, folded.shape[1]) for i in range(2)]


def per_device(
    residual,
    lengths,
    token_adapter_index,
    attention_norm_gain,
    query_key_weight,
    value_weight,
    head_second_weight,
    output_weight,
    adapter_down_maps,
    adapter_up_maps,
    feedforward_norm_gain,
    gate_weight,
    up_weight,
    down_weight,
):
    tokens, width = residual.shape
    groups = lax.axis_size("head")
    owners = lax.axis_size(BLK)
    own_width = width // groups
    own_begin = lax.axis_index("head") * own_width
    units = gate_weight.shape[1]
    qk_width = query_key_weight.shape[1]
    value_width = value_weight.shape[1]

    down_map = fold_map(adapter_down_maps[0].T)
    up_map = fold_map(lax.dynamic_slice_in_dim(adapter_up_maps[0], own_begin, own_width, 1))

    acts_local = jnp.concatenate([gate_weight, up_weight, down_weight], axis=1)
    acts_paired = lax.ppermute(acts_local, "head", [(i, i ^ 1) for i in range(groups)])
    late = lax.all_gather(
        jnp.concatenate(
            [
                acts_local[:, : 2 * units],
                acts_paired[:, : 2 * units],
                up_map,
                acts_local[:, 2 * units :],
                acts_paired[:, 2 * units :],
            ],
            axis=1,
        ),
        BLK,
        axis=0,
        tiled=True,
    )

    early = jnp.concatenate([query_key_weight, value_weight, output_weight, down_map], axis=1)
    early_width = early.shape[1]
    mine = spread(spread(early, "z"), "x")
    other = sibling(mine)
    first = lax.axis_index("core") == 0
    both = jnp.stack([jnp.where(first, mine, other), jnp.where(first, other, mine)], axis=2)
    both = both.transpose(1, 0, 2, 3, 4).reshape(width, early_width)
    qk_full = both[:, :qk_width]
    value_full = both[:, qk_width : qk_width + value_width]
    out_full = both[:, qk_width + value_width : qk_width + 2 * value_width]
    down_maps = unfold_map(both[:, qk_width + 2 * value_width :], owners)

    inputs = residual.astype(jnp.float32)
    normed = (rms_scale(inputs, 1e-06) * attention_norm_gain).astype(jnp.bfloat16)
    qk_head = jnp.dot(normed, qk_full, preferred_element_type=jnp.float32)
    value_head = jnp.dot(normed, value_full, preferred_element_type=jnp.float32).astype(jnp.bfloat16)
    allowed = request_mask(lengths[0], tokens)
    head_out = diff_head(qk_head, value_head, allowed, head_second_weight[0])

    coordinate = jnp.arange(owners * RANK, dtype=jnp.int32)
    chosen = coordinate[None, :] // RANK == token_adapter_index
    lift = (jnp.arange(RANK, dtype=jnp.int32)[:, None] == coordinate[None, :] % RANK)
    half = value_width // 2
    all_coordinates = sum(
        lax.dot_general(
            head_out[:, i * half : (i + 1) * half],
            down_maps[i],
            (((1,), (1,)), ((), ())),
            preferred_element_type=jnp.float32,
        )
        for i in range(2)
    )
    low_part = lax.dot_general(
        lift.astype(jnp.float32),
        jnp.where(chosen, all_coordinates, 0.0),
        (((1,), (1,)), ((), ())),
        precision=lax.Precision.HIGHEST,
    )
    low_high = lax.reduce_precision(low_part, 8, 7)
    low_rows = jnp.concatenate([low_high, low_part - low_high], axis=0).astype(jnp.bfloat16)
    low_rows = jnp.pad(low_rows, ((0, 0), (0, own_width - tokens)))

    share = lax.dot_general(
        head_out, out_full, (((1,), (1,)), ((), ())), preferred_element_type=jnp.float32
    ).astype(jnp.bfloat16)
    share = share.reshape(tokens, groups, own_width).transpose(1, 0, 2)
    sent = jnp.concatenate(
        [share, jnp.broadcast_to(low_rows[None], (groups, *low_rows.shape))], axis=1
    )
    total = jnp.sum(exchange(sent, "head").astype(jnp.float32), axis=0)
    low_rank = (total[tokens : tokens + RANK, :tokens] + total[tokens + RANK :, :tokens]).astype(
        jnp.bfloat16
    )
    lifted = lax.dot_general(
        low_rank,
        lift.astype(jnp.bfloat16),
        (((0,), (0,)), ((), ())),
        preferred_element_type=jnp.float32,
    )
    routed = jnp.where(chosen, lifted, 0.0).astype(jnp.bfloat16)
    up_maps = unfold_map(late[:, 4 * units : 4 * units + own_width // 2], owners)
    delta_own = (
        adapter_scaling
        * jnp.concatenate(
            [jnp.dot(routed, part, preferred_element_type=jnp.float32) for part in up_maps], axis=1
        )
    ).astype(jnp.bfloat16)
    own_mid = (
        lax.dynamic_slice_in_dim(inputs, own_begin, own_width, 1)
        + total[:tokens]
        + delta_own.astype(jnp.float32)
    )
    part = tokens // 2
    halves = own_mid.astype(jnp.bfloat16).reshape(1, 2, part, own_width)
    halves = jnp.broadcast_to(halves, (groups // 2, 2, part, own_width))
    mid_full = exchange(halves.reshape(groups, part, own_width), "head")
    mid_full = mid_full.transpose(1, 0, 2).reshape(part, width)
    ffn_in = (rms_scale(mid_full.astype(jnp.float32), 1e-06) * feedforward_norm_gain).astype(
        jnp.bfloat16
    )
    acts = jnp.dot(ffn_in, late[:, : 4 * units], preferred_element_type=jnp.float32)
    hidden_units = jnp.concatenate(
        [
            jax.nn.silu(acts[:, i * units : (i + 1) * units])
            * acts[:, (i + 1) * units : (i + 2) * units]
            for i in (0, 2)
        ],
        axis=1,
    ).astype(jnp.bfloat16)
    piece = lax.dot_general(
        hidden_units,
        late[:, 4 * units + own_width // 2 :],
        (((1,), (1,)), ((), ())),
        preferred_element_type=jnp.float32,
    ).astype(jnp.bfloat16)
    piece = piece.reshape(part, groups, own_width).transpose(1, 0, 2)
    pieces = exchange(piece, "head").reshape(groups // 2, tokens, own_width)
    return (own_mid + jnp.sum(pieces.astype(jnp.float32), axis=0)).astype(jnp.bfloat16)


def solution(mesh):
    fine = Mesh(mesh.devices.reshape(mesh.devices.shape[0], 8, 4, 2), ("head", *BLK))
    return jax.shard_map(
        per_device,
        mesh=fine,
        in_specs=(
            P(BLK, None),
            P(BLK, None),
            P(BLK, None),
            P(),
            P(BLK, "head"),
            P(BLK, "head"),
            P("head"),
            P(BLK, "head"),
            P(BLK, "head", None),
            P(BLK, None, None),
            P(),
            P(BLK, "head"),
            P(BLK, "head"),
            P(BLK, "head"),
        ),
        out_specs=P(BLK, "head"),
        check_vma=False,
    )
```

```python
import jax
import jax.numpy as jnp
from jax import lax
from jax.experimental import pallas as pl
from jax.experimental.pallas import tpu as pltpu
from jax.sharding import Mesh
from jax.sharding import PartitionSpec as P

HD = 128
RANK = 16

adapter_scaling = 2.0
head_shrink = 0.8
neg_large = -1e30

BLK = ("z", "x", "core")


def rms_scale(values, epsilon):
    return values * lax.rsqrt(jnp.mean(values * values, axis=-1, keepdims=True) + epsilon)


def nt_dot(left, right, precision=None):
    return lax.dot_general(
        left,
        right,
        (((1,), (1,)), ((), ())),
        precision=precision,
        preferred_element_type=jnp.float32,
    )


def masked_softmax(scores, allowed):
    scores = jnp.where(allowed, scores, neg_large)
    row_peak = jnp.max(scores, axis=-1, keepdims=True)
    raised = jnp.where(allowed, jnp.exp(scores - row_peak), 0.0)
    return raised / jnp.sum(raised, axis=-1, keepdims=True)


def attention_kernel(
    lengths_ref, lambda_ref, core_ref, residual_ref, gain_ref, chosen_ref, mine_ref, other_ref, sent_ref
):
    slabs_x, slabs_z, rows, width = mine_ref.shape
    tokens = residual_ref.shape[0]
    value_width = 2 * HD
    qkv_width = 4 * HD + value_width
    out_end = qkv_width + value_width
    adapters = 2 * slabs_x * slabs_z

    def body(even_ref, odd_ref):
        def gather(z, begin, end, first_row=0, last_row=rows):
            return jnp.concatenate(
                [
                    ref[x, z, first_row:last_row, begin:end]
                    for x in range(slabs_x)
                    for ref in (even_ref, odd_ref)
                ],
                axis=0,
            )

        slab = 2 * slabs_x * rows
        normed = (rms_scale(residual_ref[...].astype(jnp.float32), 1e-06) * gain_ref[...]).astype(
            jnp.bfloat16
        )
        qkv = jnp.zeros((tokens, qkv_width), jnp.float32)
        for z in range(slabs_z):
            qkv = qkv + jnp.dot(
                normed[:, z * slab : (z + 1) * slab],
                gather(z, 0, qkv_width),
                preferred_element_type=jnp.float32,
            )
        row_at = lax.broadcasted_iota(jnp.int32, (tokens, tokens), 0)
        column_at = lax.broadcasted_iota(jnp.int32, (tokens, tokens), 1)
        row_request = jnp.zeros((tokens, tokens), jnp.int32)
        column_request = jnp.zeros((tokens, tokens), jnp.int32)
        end = jnp.int32(0)
        for i in range(lengths_ref.shape[1]):
            end = end + lengths_ref[0, i]
            row_request = row_request + jnp.where(row_at >= end, 1, 0)
            column_request = column_request + jnp.where(column_at >= end, 1, 0)
        allowed = (row_request == column_request) & (column_at <= row_at)
        parts = [qkv[:, i * HD : (i + 1) * HD] for i in range(4)]
        scale = 1.0 / HD**0.5
        probs = [
            masked_softmax(nt_dot(parts[i], parts[i + 2], lax.Precision.HIGHEST) * scale, allowed)
            for i in range(2)
        ]
        mixed = (probs[0] - lambda_ref[0] * probs[1]).astype(jnp.bfloat16)
        attended = jnp.dot(
            mixed, qkv[:, 4 * HD :].astype(jnp.bfloat16), preferred_element_type=jnp.float32
        )
        head_out = (rms_scale(attended, 1e-05) * head_shrink).astype(jnp.bfloat16)

        coordinates = jnp.zeros((tokens, adapters * RANK), jnp.float32)
        for half in range(2):
            maps = jnp.concatenate(
                [
                    gather(z, out_end, width, half * RANK, (half + 1) * RANK)
                    for z in range(slabs_z)
                ],
                axis=0,
            )
            coordinates = coordinates + nt_dot(head_out[:, half * HD : (half + 1) * HD], maps)
        owner = lax.broadcasted_iota(jnp.int32, coordinates.shape, 1) // RANK
        kept = jnp.where(owner == chosen_ref[...], coordinates, 0.0)
        room = jnp.zeros((value_width - tokens, adapters * RANK), jnp.float32)
        kept = jnp.concatenate([kept, room], axis=0)
        high = kept.astype(jnp.bfloat16)
        low = (kept - high.astype(jnp.float32)).astype(jnp.bfloat16)
        lift_shape = (RANK, adapters * RANK)
        lift = jnp.where(
            lax.broadcasted_iota(jnp.int32, lift_shape, 1) % RANK
            == lax.broadcasted_iota(jnp.int32, lift_shape, 0),
            1.0,
            0.0,
        ).astype(jnp.bfloat16)
        low_rows = jnp.concatenate([nt_dot(lift, high), nt_dot(lift, low)], axis=0).astype(
            jnp.bfloat16
        )
        for z in range(slabs_z):
            sent_ref[z, :tokens, :] = nt_dot(head_out, gather(z, qkv_width, out_end)).astype(
                jnp.bfloat16
            )
            sent_ref[z, tokens:, :] = low_rows

    @pl.when(core_ref[0] == 0)
    def _():
        body(mine_ref, other_ref)

    @pl.when(core_ref[0] != 0)
    def _():
        body(other_ref, mine_ref)


def attention(lengths, second_weight, core, residual, gain, chosen, mine, other):
    tokens = residual.shape[0]
    groups = mine.shape[1]
    smem = pl.BlockSpec(memory_space=pltpu.SMEM)
    vmem = pl.BlockSpec(memory_space=pltpu.VMEM)
    return pl.pallas_call(
        attention_kernel,
        out_shape=jax.ShapeDtypeStruct((groups, tokens + 2 * RANK, 2 * HD), jnp.bfloat16),
        in_specs=[smem] * 3 + [vmem] * 5,
        out_specs=vmem,
        compiler_params=pltpu.CompilerParams(vmem_limit_bytes=48 * 1024 * 1024),
        cost_estimate=pl.CostEstimate(
            flops=1_200_000_000, bytes_accessed=8_000_000, transcendentals=80_000
        ),
    )(lengths, second_weight, core, residual, gain.reshape(1, -1), chosen, mine, other)


def exchange(blocks, axis):
    return lax.all_to_all(blocks, axis, split_axis=0, concat_axis=0, tiled=True)


def spread(block, axis):
    return exchange(jnp.broadcast_to(block[None], (lax.axis_size(axis), *block.shape)), axis)


def sibling(block):
    return lax.ppermute(block, "core", [(0, 1), (1, 0)])


def fold_map(rank_rows):
    half = rank_rows.shape[1] // 2
    return jnp.concatenate([rank_rows[:, :half], rank_rows[:, half:]], axis=0)


def unfold_map(folded, owners):
    stacked = folded.reshape(owners, 2, RANK, folded.shape[1])
    return [stacked[:, i].reshape(owners * RANK, folded.shape[1]) for i in range(2)]


def per_device(
    residual,
    lengths,
    token_adapter_index,
    attention_norm_gain,
    query_key_weight,
    value_weight,
    head_second_weight,
    output_weight,
    adapter_down_maps,
    adapter_up_maps,
    feedforward_norm_gain,
    gate_weight,
    up_weight,
    down_weight,
):
    tokens, width = residual.shape
    groups = lax.axis_size("head")
    owners = lax.axis_size(BLK)
    own_width = width // groups
    own_begin = lax.axis_index("head") * own_width
    units = gate_weight.shape[1]

    down_map = fold_map(adapter_down_maps[0].T)
    up_map = fold_map(lax.dynamic_slice_in_dim(adapter_up_maps[0], own_begin, own_width, 1))

    early = jnp.concatenate([query_key_weight, value_weight, output_weight, down_map], axis=1)
    columns = spread(early, "z")
    late_rows = jnp.concatenate([gate_weight, up_weight, up_map, down_weight], axis=1)
    columns, late_rows = lax.optimization_barrier((columns, late_rows))
    late = lax.all_gather(late_rows, BLK, axis=0, tiled=True)
    mine = spread(columns, "x")
    other = sibling(mine)
    core = lax.axis_index("core").astype(jnp.int32).reshape(1)
    sent = attention(
        lengths,
        head_second_weight,
        core,
        residual,
        attention_norm_gain,
        token_adapter_index,
        mine,
        other,
    )

    inputs = residual.astype(jnp.float32)
    coordinate = jnp.arange(owners * RANK, dtype=jnp.int32)
    chosen = coordinate[None, :] // RANK == token_adapter_index
    lift = (jnp.arange(RANK, dtype=jnp.int32)[:, None] == coordinate[None, :] % RANK)
    total = jnp.sum(exchange(sent, "head").astype(jnp.float32), axis=0)
    low_rank = (total[tokens : tokens + RANK, :tokens] + total[tokens + RANK :, :tokens]).astype(
        jnp.bfloat16
    )
    lifted = lax.dot_general(
        low_rank,
        lift.astype(jnp.bfloat16),
        (((0,), (0,)), ((), ())),
        preferred_element_type=jnp.float32,
    )
    routed = jnp.where(chosen, lifted, 0.0).astype(jnp.bfloat16)
    up_maps = unfold_map(late[:, 2 * units : 2 * units + own_width // 2], owners)
    delta_own = (
        adapter_scaling
        * jnp.concatenate(
            [jnp.dot(routed, part, preferred_element_type=jnp.float32) for part in up_maps], axis=1
        )
    ).astype(jnp.bfloat16)
    own_mid = (
        lax.dynamic_slice_in_dim(inputs, own_begin, own_width, 1)
        + total[:tokens]
        + delta_own.astype(jnp.float32)
    )
    mid_full = spread(own_mid.astype(jnp.bfloat16), "head").transpose(1, 0, 2).reshape(tokens, width)
    ffn_in = (rms_scale(mid_full.astype(jnp.float32), 1e-06) * feedforward_norm_gain).astype(
        jnp.bfloat16
    )
    both_acts = jnp.dot(ffn_in, late[:, : 2 * units], preferred_element_type=jnp.float32)
    hidden_units = (jax.nn.silu(both_acts[:, :units]) * both_acts[:, units:]).astype(jnp.bfloat16)
    piece = lax.dot_general(
        hidden_units,
        late[:, 2 * units + own_width // 2 :],
        (((1,), (1,)), ((), ())),
        preferred_element_type=jnp.float32,
    ).astype(jnp.bfloat16)
    piece = piece.reshape(tokens, groups, own_width).transpose(1, 0, 2)
    return (own_mid + jnp.sum(exchange(piece, "head").astype(jnp.float32), axis=0)).astype(
        jnp.bfloat16
    )


def solution(mesh):
    fine = Mesh(mesh.devices.reshape(mesh.devices.shape[0], 8, 4, 2), ("head", *BLK))
    return jax.shard_map(
        per_device,
        mesh=fine,
        in_specs=(
            P(BLK, None),
            P(BLK, None),
            P(BLK, None),
            P(),
            P(BLK, "head"),
            P(BLK, "head"),
            P("head"),
            P(BLK, "head"),
            P(BLK, "head", None),
            P(BLK, None, None),
            P(),
            P(BLK, "head"),
            P(BLK, "head"),
            P(BLK, "head"),
        ),
        out_specs=P(BLK, "head"),
        check_vma=False,
    )
```

```python
import jax
import jax.numpy as jnp
from jax import lax
from jax.experimental import pallas as pl
from jax.experimental.pallas import tpu as pltpu
from jax.sharding import Mesh
from jax.sharding import PartitionSpec as P

HD = 128
RANK = 16

adapter_scaling = 2.0
head_shrink = 0.8
neg_large = -1e30

BLK = ("z", "x", "core")


def rms_scale(values, epsilon):
    return values * lax.rsqrt(jnp.mean(values * values, axis=-1, keepdims=True) + epsilon)


def nt_dot(left, right, precision=None):
    return lax.dot_general(
        left,
        right,
        (((1,), (1,)), ((), ())),
        precision=precision,
        preferred_element_type=jnp.float32,
    )


def masked_softmax(scores, allowed):
    scores = jnp.where(allowed, scores, neg_large)
    row_peak = jnp.max(scores, axis=-1, keepdims=True)
    raised = jnp.where(allowed, jnp.exp(scores - row_peak), 0.0)
    return raised / jnp.sum(raised, axis=-1, keepdims=True)


def attention_kernel(
    lengths_ref, lambda_ref, core_ref, residual_ref, gain_ref, chosen_ref, mine_ref, other_ref, sent_ref
):
    slabs_x, slabs_z, rows, width = mine_ref.shape
    tokens = residual_ref.shape[0]
    value_width = 2 * HD
    qkv_width = 4 * HD + value_width
    out_end = qkv_width + value_width
    adapters = 2 * slabs_x * slabs_z

    def body(even_ref, odd_ref):
        def gather(z, begin, end, first_row=0, last_row=rows):
            return jnp.concatenate(
                [
                    ref[x, z, first_row:last_row, begin:end]
                    for x in range(slabs_x)
                    for ref in (even_ref, odd_ref)
                ],
                axis=0,
            )

        slab = 2 * slabs_x * rows
        normed = (rms_scale(residual_ref[...].astype(jnp.float32), 1e-06) * gain_ref[...]).astype(
            jnp.bfloat16
        )
        qkv = jnp.zeros((tokens, qkv_width), jnp.float32)
        for z in range(slabs_z):
            qkv = qkv + jnp.dot(
                normed[:, z * slab : (z + 1) * slab],
                gather(z, 0, qkv_width),
                preferred_element_type=jnp.float32,
            )
        row_at = lax.broadcasted_iota(jnp.int32, (tokens, tokens), 0)
        column_at = lax.broadcasted_iota(jnp.int32, (tokens, tokens), 1)
        row_request = jnp.zeros((tokens, tokens), jnp.int32)
        column_request = jnp.zeros((tokens, tokens), jnp.int32)
        end = jnp.int32(0)
        for i in range(lengths_ref.shape[1]):
            end = end + lengths_ref[0, i]
            row_request = row_request + jnp.where(row_at >= end, 1, 0)
            column_request = column_request + jnp.where(column_at >= end, 1, 0)
        allowed = (row_request == column_request) & (column_at <= row_at)
        parts = [qkv[:, i * HD : (i + 1) * HD] for i in range(4)]
        scale = 1.0 / HD**0.5
        probs = [
            masked_softmax(nt_dot(parts[i], parts[i + 2], lax.Precision.HIGHEST) * scale, allowed)
            for i in range(2)
        ]
        mixed = (probs[0] - lambda_ref[0] * probs[1]).astype(jnp.bfloat16)
        attended = jnp.dot(
            mixed, qkv[:, 4 * HD :].astype(jnp.bfloat16), preferred_element_type=jnp.float32
        )
        head_out = (rms_scale(attended, 1e-05) * head_shrink).astype(jnp.bfloat16)

        coordinates = jnp.zeros((tokens, adapters * RANK), jnp.float32)
        for half in range(2):
            maps = jnp.concatenate(
                [
                    gather(z, out_end, width, half * RANK, (half + 1) * RANK)
                    for z in range(slabs_z)
                ],
                axis=0,
            )
            coordinates = coordinates + nt_dot(head_out[:, half * HD : (half + 1) * HD], maps)
        owner = lax.broadcasted_iota(jnp.int32, coordinates.shape, 1) // RANK
        kept = jnp.where(owner == chosen_ref[...], coordinates, 0.0)
        room = jnp.zeros((value_width - tokens, adapters * RANK), jnp.float32)
        kept = jnp.concatenate([kept, room], axis=0)
        high = kept.astype(jnp.bfloat16)
        low = (kept - high.astype(jnp.float32)).astype(jnp.bfloat16)
        lift_shape = (RANK, adapters * RANK)
        lift = jnp.where(
            lax.broadcasted_iota(jnp.int32, lift_shape, 1) % RANK
            == lax.broadcasted_iota(jnp.int32, lift_shape, 0),
            1.0,
            0.0,
        ).astype(jnp.bfloat16)
        low_rows = jnp.concatenate([nt_dot(lift, high), nt_dot(lift, low)], axis=0).astype(
            jnp.bfloat16
        )
        for z in range(slabs_z):
            sent_ref[z, :tokens, :] = nt_dot(head_out, gather(z, qkv_width, out_end)).astype(
                jnp.bfloat16
            )
            sent_ref[z, tokens:, :] = low_rows

    @pl.when(core_ref[0] == 0)
    def _():
        body(mine_ref, other_ref)

    @pl.when(core_ref[0] != 0)
    def _():
        body(other_ref, mine_ref)


def attention(lengths, second_weight, core, residual, gain, chosen, mine, other):
    tokens = residual.shape[0]
    groups = mine.shape[1]
    smem = pl.BlockSpec(memory_space=pltpu.SMEM)
    vmem = pl.BlockSpec(memory_space=pltpu.VMEM)
    return pl.pallas_call(
        attention_kernel,
        out_shape=jax.ShapeDtypeStruct((groups, tokens + 2 * RANK, 2 * HD), jnp.bfloat16),
        in_specs=[smem] * 3 + [vmem] * 5,
        out_specs=vmem,
        compiler_params=pltpu.CompilerParams(vmem_limit_bytes=48 * 1024 * 1024),
        cost_estimate=pl.CostEstimate(
            flops=1_200_000_000, bytes_accessed=8_000_000, transcendentals=80_000
        ),
    )(lengths, second_weight, core, residual, gain.reshape(1, -1), chosen, mine, other)


def exchange(blocks, axis):
    return lax.all_to_all(blocks, axis, split_axis=0, concat_axis=0, tiled=True)


def spread(block, axis):
    return exchange(jnp.broadcast_to(block[None], (lax.axis_size(axis), *block.shape)), axis)


def sibling(block):
    return lax.ppermute(block, "core", [(0, 1), (1, 0)])


def fold_map(rank_rows):
    half = rank_rows.shape[1] // 2
    return jnp.concatenate([rank_rows[:, :half], rank_rows[:, half:]], axis=0)


def unfold_map(folded, owners):
    stacked = folded.reshape(owners, 2, RANK, folded.shape[1])
    return [stacked[:, i].reshape(owners * RANK, folded.shape[1]) for i in range(2)]


def per_device(
    residual,
    lengths,
    token_adapter_index,
    attention_norm_gain,
    query_key_weight,
    value_weight,
    head_second_weight,
    output_weight,
    adapter_down_maps,
    adapter_up_maps,
    feedforward_norm_gain,
    gate_weight,
    up_weight,
    down_weight,
):
    tokens, width = residual.shape
    groups = lax.axis_size("head")
    owners = lax.axis_size(BLK)
    own_width = width // groups
    own_begin = lax.axis_index("head") * own_width
    units = gate_weight.shape[1]

    down_map = fold_map(adapter_down_maps[0].T)
    up_map = fold_map(lax.dynamic_slice_in_dim(adapter_up_maps[0], own_begin, own_width, 1))

    early = jnp.concatenate([query_key_weight, value_weight, output_weight, down_map], axis=1)
    late_rows = jnp.concatenate([gate_weight, up_weight, up_map, down_weight], axis=1)
    late = lax.all_gather(late_rows, BLK, axis=0, tiled=True)
    mine = spread(spread(early, "z"), "x")
    other = sibling(mine)
    core = lax.axis_index("core").astype(jnp.int32).reshape(1)
    sent = attention(
        lengths,
        head_second_weight,
        core,
        residual,
        attention_norm_gain,
        token_adapter_index,
        mine,
        other,
    )

    inputs = residual.astype(jnp.float32)
    coordinate = jnp.arange(owners * RANK, dtype=jnp.int32)
    chosen = coordinate[None, :] // RANK == token_adapter_index
    lift = (jnp.arange(RANK, dtype=jnp.int32)[:, None] == coordinate[None, :] % RANK)
    total = jnp.sum(exchange(sent, "head").astype(jnp.float32), axis=0)
    low_rank = (total[tokens : tokens + RANK, :tokens] + total[tokens + RANK :, :tokens]).astype(
        jnp.bfloat16
    )
    lifted = lax.dot_general(
        low_rank,
        lift.astype(jnp.bfloat16),
        (((0,), (0,)), ((), ())),
        preferred_element_type=jnp.float32,
    )
    routed = jnp.where(chosen, lifted, 0.0).astype(jnp.bfloat16)
    up_maps = unfold_map(late[:, 2 * units : 2 * units + own_width // 2], owners)
    delta_own = (
        adapter_scaling
        * jnp.concatenate(
            [jnp.dot(routed, part, preferred_element_type=jnp.float32) for part in up_maps], axis=1
        )
    ).astype(jnp.bfloat16)
    own_mid = (
        lax.dynamic_slice_in_dim(inputs, own_begin, own_width, 1)
        + total[:tokens]
        + delta_own.astype(jnp.float32)
    )
    mid_full = spread(own_mid.astype(jnp.bfloat16), "head").transpose(1, 0, 2).reshape(tokens, width)
    ffn_in = (rms_scale(mid_full.astype(jnp.float32), 1e-06) * feedforward_norm_gain).astype(
        jnp.bfloat16
    )
    both_acts = jnp.dot(ffn_in, late[:, : 2 * units], preferred_element_type=jnp.float32)
    hidden_units = (jax.nn.silu(both_acts[:, :units]) * both_acts[:, units:]).astype(jnp.bfloat16)
    piece = lax.dot_general(
        hidden_units,
        late[:, 2 * units + own_width // 2 :],
        (((1,), (1,)), ((), ())),
        preferred_element_type=jnp.float32,
    ).astype(jnp.bfloat16)
    piece = piece.reshape(tokens, groups, own_width).transpose(1, 0, 2)
    return (own_mid + jnp.sum(exchange(piece, "head").astype(jnp.float32), axis=0)).astype(
        jnp.bfloat16
    )


def solution(mesh):
    fine = Mesh(mesh.devices.reshape(mesh.devices.shape[0], 8, 4, 2), ("head", *BLK))
    return jax.shard_map(
        per_device,
        mesh=fine,
        in_specs=(
            P(BLK, None),
            P(BLK, None),
            P(BLK, None),
            P(),
            P(BLK, "head"),
            P(BLK, "head"),
            P("head"),
            P(BLK, "head"),
            P(BLK, "head", None),
            P(BLK, None, None),
            P(),
            P(BLK, "head"),
            P(BLK, "head"),
            P(BLK, "head"),
        ),
        out_specs=P(BLK, "head"),
        check_vma=False,
    )
```

```python
import jax
import jax.numpy as jnp
from jax import lax
from jax.experimental import pallas as pl
from jax.experimental.pallas import tpu as pltpu
from jax.sharding import Mesh
from jax.sharding import PartitionSpec as P

HD = 128
RANK = 16

adapter_scaling = 2.0
head_shrink = 0.8
neg_large = -1e30

BLK = ("z", "x", "core")


def rms_scale(values, epsilon):
    return values * lax.rsqrt(jnp.mean(values * values, axis=-1, keepdims=True) + epsilon)


def nt_dot(left, right, precision=None):
    return lax.dot_general(
        left,
        right,
        (((1,), (1,)), ((), ())),
        precision=precision,
        preferred_element_type=jnp.float32,
    )


def masked_softmax(scores, allowed):
    scores = jnp.where(allowed, scores, neg_large)
    row_peak = jnp.max(scores, axis=-1, keepdims=True)
    raised = jnp.where(allowed, jnp.exp(scores - row_peak), 0.0)
    return raised / jnp.sum(raised, axis=-1, keepdims=True)


def attention_kernel(
    lengths_ref, lambda_ref, core_ref, residual_ref, gain_ref, chosen_ref, mine_ref, other_ref, sent_ref, up_ref
):
    slabs_x, slabs_z, rows, _ = mine_ref.shape
    tokens = residual_ref.shape[0]
    value_width = 2 * HD
    qkv_width = 4 * HD + value_width
    out_end = qkv_width + value_width
    adapters = 2 * slabs_x * slabs_z

    def body(even_ref, odd_ref):
        def gather(z, begin, end, first_row=0, last_row=rows):
            return jnp.concatenate(
                [
                    ref[x, z, first_row:last_row, begin:end]
                    for x in range(slabs_x)
                    for ref in (even_ref, odd_ref)
                ],
                axis=0,
            )

        slab = 2 * slabs_x * rows
        normed = (rms_scale(residual_ref[...].astype(jnp.float32), 1e-06) * gain_ref[...]).astype(
            jnp.bfloat16
        )
        qkv = jnp.zeros((tokens, qkv_width), jnp.float32)
        for z in range(slabs_z):
            qkv = qkv + jnp.dot(
                normed[:, z * slab : (z + 1) * slab],
                gather(z, 0, qkv_width),
                preferred_element_type=jnp.float32,
            )
        row_at = lax.broadcasted_iota(jnp.int32, (tokens, tokens), 0)
        column_at = lax.broadcasted_iota(jnp.int32, (tokens, tokens), 1)
        row_request = jnp.zeros((tokens, tokens), jnp.int32)
        column_request = jnp.zeros((tokens, tokens), jnp.int32)
        end = jnp.int32(0)
        for i in range(lengths_ref.shape[1]):
            end = end + lengths_ref[0, i]
            row_request = row_request + jnp.where(row_at >= end, 1, 0)
            column_request = column_request + jnp.where(column_at >= end, 1, 0)
        allowed = (row_request == column_request) & (column_at <= row_at)
        parts = [qkv[:, i * HD : (i + 1) * HD] for i in range(4)]
        scale = 1.0 / HD**0.5
        probs = [
            masked_softmax(nt_dot(parts[i], parts[i + 2], lax.Precision.HIGHEST) * scale, allowed)
            for i in range(2)
        ]
        mixed = (probs[0] - lambda_ref[0] * probs[1]).astype(jnp.bfloat16)
        attended = jnp.dot(
            mixed, qkv[:, 4 * HD :].astype(jnp.bfloat16), preferred_element_type=jnp.float32
        )
        head_out = (rms_scale(attended, 1e-05) * head_shrink).astype(jnp.bfloat16)

        coordinates = jnp.zeros((tokens, adapters * RANK), jnp.float32)
        for half in range(2):
            folded_rows = (half * RANK, (half + 1) * RANK)
            maps = jnp.concatenate(
                [gather(z, out_end, out_end + HD, *folded_rows) for z in range(slabs_z)], axis=0
            )
            for z in range(slabs_z):
                piece = gather(z, out_end + HD, out_end + 2 * HD, *folded_rows)
                up_ref[z * piece.shape[0] : (z + 1) * piece.shape[0], half * HD : (half + 1) * HD] = (
                    piece
                )
            coordinates = coordinates + nt_dot(head_out[:, half * HD : (half + 1) * HD], maps)
        owner = lax.broadcasted_iota(jnp.int32, coordinates.shape, 1) // RANK
        kept = jnp.where(owner == chosen_ref[...], coordinates, 0.0)
        room = jnp.zeros((value_width - tokens, adapters * RANK), jnp.float32)
        kept = jnp.concatenate([kept, room], axis=0)
        high = kept.astype(jnp.bfloat16)
        low = (kept - high.astype(jnp.float32)).astype(jnp.bfloat16)
        lift_shape = (RANK, adapters * RANK)
        lift = jnp.where(
            lax.broadcasted_iota(jnp.int32, lift_shape, 1) % RANK
            == lax.broadcasted_iota(jnp.int32, lift_shape, 0),
            1.0,
            0.0,
        ).astype(jnp.bfloat16)
        low_rows = jnp.concatenate([nt_dot(lift, high), nt_dot(lift, low)], axis=0).astype(
            jnp.bfloat16
        )
        for z in range(slabs_z):
            sent_ref[z, :tokens, :] = nt_dot(head_out, gather(z, qkv_width, out_end)).astype(
                jnp.bfloat16
            )
            sent_ref[z, tokens:, :] = low_rows

    @pl.when(core_ref[0] == 0)
    def _():
        body(mine_ref, other_ref)

    @pl.when(core_ref[0] != 0)
    def _():
        body(other_ref, mine_ref)


def attention(lengths, second_weight, core, residual, gain, chosen, mine, other):
    tokens = residual.shape[0]
    groups = mine.shape[1]
    smem = pl.BlockSpec(memory_space=pltpu.SMEM)
    vmem = pl.BlockSpec(memory_space=pltpu.VMEM)
    return pl.pallas_call(
        attention_kernel,
        out_shape=[
            jax.ShapeDtypeStruct((groups, tokens + 2 * RANK, 2 * HD), jnp.bfloat16),
            jax.ShapeDtypeStruct((2 * mine.shape[0] * groups * RANK, 2 * HD), jnp.bfloat16),
        ],
        in_specs=[smem] * 3 + [vmem] * 5,
        out_specs=[vmem] * 2,
        compiler_params=pltpu.CompilerParams(vmem_limit_bytes=48 * 1024 * 1024),
        cost_estimate=pl.CostEstimate(
            flops=1_200_000_000, bytes_accessed=8_000_000, transcendentals=80_000
        ),
    )(lengths, second_weight, core, residual, gain.reshape(1, -1), chosen, mine, other)


def feed_forward_kernel(mid_ref, gain_ref, weights_ref, out_ref, normed_ref, acts_ref, hidden_ref):
    phase, step = pl.program_id(0), pl.program_id(1)
    groups, _, slab = mid_ref.shape
    pairs = weights_ref.shape[1]
    per_step = weights_ref.shape[0] // slab

    @pl.when((phase == 0) & (step == 0))
    def _():
        mid = mid_ref[...].astype(jnp.float32)
        square = jnp.sum(jnp.sum(mid * mid, axis=0), axis=-1, keepdims=True) / (groups * slab)
        scaled = mid * lax.rsqrt(square + 1e-06)[None] * gain_ref[...]
        normed_ref[...] = scaled.astype(jnp.bfloat16)

    @pl.when(phase < 2)
    def _():
        product = sum(
            jnp.dot(
                normed_ref[step * per_step + i],
                weights_ref[i * slab : (i + 1) * slab, :],
                preferred_element_type=jnp.float32,
            )
            for i in range(per_step)
        )

        @pl.when(step == 0)
        def _():
            acts_ref[...] = product

        @pl.when(step > 0)
        def _():
            acts_ref[...] += product

    last = step == pl.num_programs(1) - 1

    @pl.when(last & (phase == 0))
    def _():
        acts = acts_ref[...]
        hidden_ref[...] = jax.nn.silu(acts) * pltpu.roll(acts, pairs // 2, 1)

    @pl.when(last & (phase == 1))
    def _():
        acts = acts_ref[...]
        lane = lax.broadcasted_iota(jnp.int32, acts.shape, 1)
        hidden_ref[...] = jnp.where(
            lane < pairs // 2,
            hidden_ref[...],
            jax.nn.silu(pltpu.roll(acts, pairs // 2, 1)) * acts,
        )

    @pl.when(phase == 2)
    def _():
        hidden = hidden_ref[...].astype(jnp.bfloat16)
        for i in range(per_step):
            out_ref[i] = nt_dot(hidden, weights_ref[i * slab : (i + 1) * slab, :]).astype(jnp.bfloat16)


def feed_forward(mid, gain, weights):
    groups, part, slab = mid.shape
    width, columns = weights.shape
    pairs = columns // 3
    steps = 4
    return pl.pallas_call(
        feed_forward_kernel,
        grid=(3, steps),
        out_shape=jax.ShapeDtypeStruct(mid.shape, jnp.bfloat16),
        in_specs=[
            pl.BlockSpec(mid.shape, lambda phase, step: (0, 0, 0)),
            pl.BlockSpec((groups, 1, slab), lambda phase, step: (0, 0, 0)),
            pl.BlockSpec((width // steps, pairs), lambda phase, step: (step, phase)),
        ],
        out_specs=pl.BlockSpec(
            (groups // steps, part, slab),
            lambda phase, step: (jnp.where(phase == 2, step, 0), 0, 0),
        ),
        scratch_shapes=[
            pltpu.VMEM(mid.shape, jnp.bfloat16),
            pltpu.VMEM((part, pairs), jnp.float32),
            pltpu.VMEM((part, pairs), jnp.float32),
        ],
        compiler_params=pltpu.CompilerParams(vmem_limit_bytes=40 * 1024 * 1024),
        cost_estimate=pl.CostEstimate(
            flops=1_700_000_000, bytes_accessed=18_000_000, transcendentals=300_000
        ),
    )(mid, gain.reshape(groups, 1, slab), weights)


def exchange(blocks, axis):
    return lax.all_to_all(blocks, axis, split_axis=0, concat_axis=0, tiled=True)


def spread(block, axis):
    return exchange(jnp.broadcast_to(block[None], (lax.axis_size(axis), *block.shape)), axis)


def sibling(block):
    return lax.ppermute(block, "core", [(0, 1), (1, 0)])


def fold_map(rank_rows):
    half = rank_rows.shape[1] // 2
    return jnp.concatenate([rank_rows[:, :half], rank_rows[:, half:]], axis=0)


def per_device(
    residual,
    lengths,
    token_adapter_index,
    attention_norm_gain,
    query_key_weight,
    value_weight,
    head_second_weight,
    output_weight,
    adapter_down_maps,
    adapter_up_maps,
    feedforward_norm_gain,
    gate_weight,
    up_weight,
    down_weight,
):
    tokens, width = residual.shape
    groups = lax.axis_size("head")
    owners = lax.axis_size(BLK)
    own_width = width // groups
    own_begin = lax.axis_index("head") * own_width
    units = gate_weight.shape[1]

    down_map = fold_map(adapter_down_maps[0].T)
    up_map = fold_map(lax.dynamic_slice_in_dim(adapter_up_maps[0], own_begin, own_width, 1))

    early = jnp.concatenate([query_key_weight, value_weight, output_weight, down_map, up_map], axis=1)
    acts_own = jnp.concatenate([gate_weight, up_weight, down_weight], axis=1)
    acts_pair = lax.ppermute(acts_own, "head", [(i, i ^ 1) for i in range(groups)])
    late = lax.all_gather(
        jnp.concatenate(
            [
                acts_own[:, : 2 * units],
                acts_pair[:, : 2 * units],
                acts_own[:, 2 * units :],
                acts_pair[:, 2 * units :],
            ],
            axis=1,
        ),
        BLK,
        axis=0,
        tiled=True,
    )
    mine = spread(spread(early, "z"), "x")
    other = sibling(mine)
    core = lax.axis_index("core").astype(jnp.int32).reshape(1)
    sent, up_maps = attention(
        lengths,
        head_second_weight,
        core,
        residual,
        attention_norm_gain,
        token_adapter_index,
        mine,
        other,
    )

    inputs = residual.astype(jnp.float32)
    coordinate = jnp.arange(owners * RANK, dtype=jnp.int32)
    chosen = coordinate[None, :] // RANK == token_adapter_index
    lift = (jnp.arange(RANK, dtype=jnp.int32)[:, None] == coordinate[None, :] % RANK)
    total = jnp.sum(exchange(sent, "head").astype(jnp.float32), axis=0)
    low_rank = (total[tokens : tokens + RANK, :tokens] + total[tokens + RANK :, :tokens]).astype(
        jnp.bfloat16
    )
    lifted = lax.dot_general(
        low_rank,
        lift.astype(jnp.bfloat16),
        (((0,), (0,)), ((), ())),
        preferred_element_type=jnp.float32,
    )
    routed = jnp.where(chosen, lifted, 0.0).astype(jnp.bfloat16)
    delta_own = (
        adapter_scaling * jnp.dot(routed, up_maps, preferred_element_type=jnp.float32)
    ).astype(jnp.bfloat16)
    own_mid = (
        lax.dynamic_slice_in_dim(inputs, own_begin, own_width, 1)
        + total[:tokens]
        + delta_own.astype(jnp.float32)
    )
    part = tokens // 2
    halves = own_mid.astype(jnp.bfloat16).reshape(1, 2, part, own_width)
    halves = jnp.broadcast_to(halves, (groups // 2, 2, part, own_width))
    mid_full = exchange(halves.reshape(groups, part, own_width), "head")
    piece = feed_forward(mid_full, feedforward_norm_gain, late)
    pieces = exchange(piece, "head").reshape(groups // 2, tokens, own_width)
    return (own_mid + jnp.sum(pieces.astype(jnp.float32), axis=0)).astype(jnp.bfloat16)


def solution(mesh):
    fine = Mesh(mesh.devices.reshape(mesh.devices.shape[0], 8, 4, 2), ("head", *BLK))
    return jax.shard_map(
        per_device,
        mesh=fine,
        in_specs=(
            P(BLK, None),
            P(BLK, None),
            P(BLK, None),
            P(),
            P(BLK, "head"),
            P(BLK, "head"),
            P("head"),
            P(BLK, "head"),
            P(BLK, "head", None),
            P(BLK, None, None),
            P(),
            P(BLK, "head"),
            P(BLK, "head"),
            P(BLK, "head"),
        ),
        out_specs=P(BLK, "head"),
        check_vma=False,
    )
```

```python
import jax
import jax.numpy as jnp
from jax import lax
from jax.experimental import pallas as pl
from jax.experimental.pallas import tpu as pltpu
from jax.sharding import Mesh
from jax.sharding import PartitionSpec as P

HD = 128
RANK = 16

adapter_scaling = 2.0
head_shrink = 0.8
neg_large = -1e30

BLK = ("z", "x", "core")


def rms_scale(values, epsilon):
    return values * lax.rsqrt(jnp.mean(values * values, axis=-1, keepdims=True) + epsilon)


def nt_dot(left, right, precision=None):
    return lax.dot_general(
        left,
        right,
        (((1,), (1,)), ((), ())),
        precision=precision,
        preferred_element_type=jnp.float32,
    )


def masked_softmax(scores, allowed):
    scores = jnp.where(allowed, scores, neg_large)
    row_peak = jnp.max(scores, axis=-1, keepdims=True)
    raised = jnp.where(allowed, jnp.exp(scores - row_peak), 0.0)
    return raised / jnp.sum(raised, axis=-1, keepdims=True)


def attention_kernel(
    lengths_ref, lambda_ref, core_ref, residual_ref, gain_ref, chosen_ref, mine_ref, other_ref, sent_ref
):
    slabs_x, slabs_z, rows, _ = mine_ref.shape
    tokens = residual_ref.shape[0]
    value_width = 2 * HD
    qkv_width = 4 * HD + value_width
    out_end = qkv_width + value_width
    adapters = 2 * slabs_x * slabs_z

    def body(even_ref, odd_ref):
        def gather(z, begin, end, first_row=0, last_row=rows):
            return jnp.concatenate(
                [
                    ref[x, z, first_row:last_row, begin:end]
                    for x in range(slabs_x)
                    for ref in (even_ref, odd_ref)
                ],
                axis=0,
            )

        slab = 2 * slabs_x * rows
        normed = (rms_scale(residual_ref[...].astype(jnp.float32), 1e-06) * gain_ref[...]).astype(
            jnp.bfloat16
        )
        qkv = jnp.zeros((tokens, qkv_width), jnp.float32)
        for z in range(slabs_z):
            qkv = qkv + jnp.dot(
                normed[:, z * slab : (z + 1) * slab],
                gather(z, 0, qkv_width),
                preferred_element_type=jnp.float32,
            )
        row_at = lax.broadcasted_iota(jnp.int32, (tokens, tokens), 0)
        column_at = lax.broadcasted_iota(jnp.int32, (tokens, tokens), 1)
        row_request = jnp.zeros((tokens, tokens), jnp.int32)
        column_request = jnp.zeros((tokens, tokens), jnp.int32)
        end = jnp.int32(0)
        for i in range(lengths_ref.shape[1]):
            end = end + lengths_ref[0, i]
            row_request = row_request + jnp.where(row_at >= end, 1, 0)
            column_request = column_request + jnp.where(column_at >= end, 1, 0)
        allowed = (row_request == column_request) & (column_at <= row_at)
        parts = [qkv[:, i * HD : (i + 1) * HD] for i in range(4)]
        scale = 1.0 / HD**0.5
        probs = [
            masked_softmax(nt_dot(parts[i], parts[i + 2], lax.Precision.HIGHEST) * scale, allowed)
            for i in range(2)
        ]
        mixed = (probs[0] - lambda_ref[0] * probs[1]).astype(jnp.bfloat16)
        attended = jnp.dot(
            mixed, qkv[:, 4 * HD :].astype(jnp.bfloat16), preferred_element_type=jnp.float32
        )
        head_out = (rms_scale(attended, 1e-05) * head_shrink).astype(jnp.bfloat16)

        coordinates = jnp.zeros((tokens, adapters * RANK), jnp.float32)
        for half in range(2):
            folded_rows = (half * RANK, (half + 1) * RANK)
            maps = jnp.concatenate(
                [gather(z, out_end, out_end + HD, *folded_rows) for z in range(slabs_z)], axis=0
            )
            coordinates = coordinates + nt_dot(head_out[:, half * HD : (half + 1) * HD], maps)
        owner = lax.broadcasted_iota(jnp.int32, coordinates.shape, 1) // RANK
        kept = jnp.where(owner == chosen_ref[...], coordinates, 0.0)
        room = jnp.zeros((value_width - tokens, adapters * RANK), jnp.float32)
        kept = jnp.concatenate([kept, room], axis=0)
        high = kept.astype(jnp.bfloat16)
        low = (kept - high.astype(jnp.float32)).astype(jnp.bfloat16)
        lift_shape = (RANK, adapters * RANK)
        lift = jnp.where(
            lax.broadcasted_iota(jnp.int32, lift_shape, 1) % RANK
            == lax.broadcasted_iota(jnp.int32, lift_shape, 0),
            1.0,
            0.0,
        ).astype(jnp.bfloat16)
        low_rows = jnp.concatenate([nt_dot(lift, high), nt_dot(lift, low)], axis=0).astype(
            jnp.bfloat16
        )
        for z in range(slabs_z):
            sent_ref[z, :tokens, :] = nt_dot(head_out, gather(z, qkv_width, out_end)).astype(
                jnp.bfloat16
            )
            sent_ref[z, tokens:, :] = low_rows

    @pl.when(core_ref[0] == 0)
    def _():
        body(mine_ref, other_ref)

    @pl.when(core_ref[0] != 0)
    def _():
        body(other_ref, mine_ref)


def attention(lengths, second_weight, core, residual, gain, chosen, mine, other):
    tokens = residual.shape[0]
    groups = mine.shape[1]
    smem = pl.BlockSpec(memory_space=pltpu.SMEM)
    vmem = pl.BlockSpec(memory_space=pltpu.VMEM)
    return pl.pallas_call(
        attention_kernel,
        out_shape=jax.ShapeDtypeStruct((groups, tokens + 2 * RANK, 2 * HD), jnp.bfloat16),
        in_specs=[smem] * 3 + [vmem] * 5,
        out_specs=vmem,
        compiler_params=pltpu.CompilerParams(vmem_limit_bytes=48 * 1024 * 1024),
        cost_estimate=pl.CostEstimate(
            flops=1_200_000_000, bytes_accessed=8_000_000, transcendentals=80_000
        ),
    )(lengths, second_weight, core, residual, gain.reshape(1, -1), chosen, mine, other)


def middle_kernel(core_ref, chosen_ref, residual_ref, received_ref, mine_ref, other_ref, mid_ref, sent_ref):
    slabs_x, slabs_z, _, half_width = mine_ref.shape
    tokens = chosen_ref.shape[0]
    part = tokens // 2
    adapters = 2 * slabs_x * slabs_z

    def body(even_ref, odd_ref):
        total = received_ref[0].astype(jnp.float32)
        for group in range(1, received_ref.shape[0]):
            total = total + received_ref[group].astype(jnp.float32)
        low_rank = (total[tokens : tokens + RANK] + total[tokens + RANK :]).astype(jnp.bfloat16)
        lift_shape = (RANK, adapters * RANK)
        lift = jnp.where(
            lax.broadcasted_iota(jnp.int32, lift_shape, 1) % RANK
            == lax.broadcasted_iota(jnp.int32, lift_shape, 0),
            1.0,
            0.0,
        ).astype(jnp.bfloat16)
        lifted = lax.dot_general(
            low_rank, lift, (((0,), (0,)), ((), ())), preferred_element_type=jnp.float32
        )[:tokens]
        owner = lax.broadcasted_iota(jnp.int32, lifted.shape, 1) // RANK
        routed = jnp.where(owner == chosen_ref[...], lifted, 0.0).astype(jnp.bfloat16)
        for half in range(2):
            maps = jnp.concatenate(
                [
                    ref[x, z, half * RANK : (half + 1) * RANK, :]
                    for z in range(slabs_z)
                    for x in range(slabs_x)
                    for ref in (even_ref, odd_ref)
                ],
                axis=0,
            )
            delta = (
                adapter_scaling * jnp.dot(routed, maps, preferred_element_type=jnp.float32)
            ).astype(jnp.bfloat16)
            lanes = slice(half * half_width, (half + 1) * half_width)
            mid = residual_ref[:, lanes].astype(jnp.float32) + total[:tokens, lanes]
            mid_ref[:, lanes] = mid + delta.astype(jnp.float32)
        rounded = mid_ref[...].astype(jnp.bfloat16)
        for group in range(sent_ref.shape[0]):
            side = group % 2
            sent_ref[group] = rounded[side * part : (side + 1) * part]

    @pl.when(core_ref[0] == 0)
    def _():
        body(mine_ref, other_ref)

    @pl.when(core_ref[0] != 0)
    def _():
        body(other_ref, mine_ref)


def middle(core, chosen, residual, received, mine, other):
    tokens, own_width = residual.shape
    groups = received.shape[0]
    last = mine.shape[3] // HD - 1
    vmem = pl.BlockSpec(memory_space=pltpu.VMEM)
    maps = pl.BlockSpec((*mine.shape[:3], HD), lambda i: (0, 0, 0, last))

    def whole(array):
        return pl.BlockSpec(array.shape, lambda i: (0,) * len(array.shape))

    return pl.pallas_call(
        middle_kernel,
        grid=(1,),
        out_shape=[
            jax.ShapeDtypeStruct((tokens, own_width), jnp.float32),
            jax.ShapeDtypeStruct((groups, tokens // 2, own_width), jnp.bfloat16),
        ],
        in_specs=[
            pl.BlockSpec(memory_space=pltpu.SMEM),
            whole(chosen),
            whole(residual),
            whole(received),
            maps,
            maps,
        ],
        out_specs=[
            pl.BlockSpec((tokens, own_width), lambda i: (0, 0)),
            pl.BlockSpec((groups, tokens // 2, own_width), lambda i: (0, 0, 0)),
        ],
        compiler_params=pltpu.CompilerParams(vmem_limit_bytes=32 * 1024 * 1024),
        cost_estimate=pl.CostEstimate(
            flops=120_000_000, bytes_accessed=3_000_000, transcendentals=0
        ),
    )(core, chosen, residual, received, mine, other)


def feed_forward_kernel(mid_ref, gain_ref, weights_ref, out_ref, acts_ref, down_ref, acts_in, down_in):
    sides, steps, owners, rows, pairs = acts_ref.shape
    padded = down_ref.shape[4]
    groups, _, slab = mid_ref.shape
    units = pairs // 2
    per_step = owners * rows // slab

    def fetch(side, step, begin, count, held_ref, arrived):
        return pltpu.make_async_copy(
            weights_ref.at[pl.ds(step * owners, owners), side, :, pl.ds(begin, count)],
            held_ref.at[side, step],
            arrived.at[side, step],
        )

    acts_copies = [
        [fetch(side, step, 0, pairs, acts_ref, acts_in) for step in range(steps)]
        for side in range(sides)
    ]
    down_copies = [
        [fetch(side, step, pairs, padded, down_ref, down_in) for side in range(sides)]
        for step in range(steps)
    ]
    for row in acts_copies + down_copies:
        for copy in row:
            copy.start()
    mid = mid_ref[...].astype(jnp.float32)
    square = jnp.sum(jnp.sum(mid * mid, axis=0), axis=-1, keepdims=True) / (groups * slab)
    normed = (mid * lax.rsqrt(square + 1e-06)[None] * gain_ref[...]).astype(jnp.bfloat16)

    hidden = []
    for side in range(sides):
        acts = None
        for step in range(steps):
            left = jnp.concatenate(
                [normed[step * per_step + i] for i in range(per_step)], axis=1
            )
            acts_copies[side][step].wait()
            product = jnp.dot(
                left,
                acts_ref[side, step].reshape(owners * rows, pairs),
                preferred_element_type=jnp.float32,
            )
            acts = product if acts is None else acts + product
        upward = pltpu.roll(acts, units, 1)[:, :padded]
        lane = lax.broadcasted_iota(jnp.int32, upward.shape, 1)
        gated = jax.nn.silu(acts[:, :padded]) * upward
        hidden.append(jnp.where(lane < units, gated, 0.0).astype(jnp.bfloat16))
    for step in range(steps):
        for copy in down_copies[step]:
            copy.wait()
        for i in range(per_step):
            picked = slice(i * slab, (i + 1) * slab)
            out_ref[step * per_step + i] = sum(
                nt_dot(
                    hidden[side], down_ref[side, step].reshape(owners * rows, padded)[picked]
                )
                for side in range(sides)
            ).astype(jnp.bfloat16)


def feed_forward(mid, gain, weights, units):
    groups, _, slab = mid.shape
    owners, sides, rows, columns = weights.shape
    steps = 4
    held = (sides, steps, owners // steps, rows)
    vmem = pl.BlockSpec(memory_space=pltpu.VMEM)
    return pl.pallas_call(
        feed_forward_kernel,
        out_shape=jax.ShapeDtypeStruct(mid.shape, jnp.bfloat16),
        in_specs=[vmem, vmem, pl.BlockSpec(memory_space=pl.ANY)],
        out_specs=vmem,
        scratch_shapes=[
            pltpu.VMEM((*held, 2 * units), jnp.bfloat16),
            pltpu.VMEM((*held, columns - 2 * units), jnp.bfloat16),
            pltpu.SemaphoreType.DMA((sides, steps)),
            pltpu.SemaphoreType.DMA((sides, steps)),
        ],
        compiler_params=pltpu.CompilerParams(vmem_limit_bytes=40 * 1024 * 1024),
        cost_estimate=pl.CostEstimate(
            flops=1_700_000_000, bytes_accessed=18_000_000, transcendentals=300_000
        ),
    )(mid, gain.reshape(groups, 1, slab), weights)


def exchange(blocks, axis):
    return lax.all_to_all(blocks, axis, split_axis=0, concat_axis=0, tiled=True)


def spread(block, axis):
    return exchange(jnp.broadcast_to(block[None], (lax.axis_size(axis), *block.shape)), axis)


def sibling(block):
    return lax.ppermute(block, "core", [(0, 1), (1, 0)])


def fold_map(rank_rows):
    half = rank_rows.shape[1] // 2
    return jnp.concatenate([rank_rows[:, :half], rank_rows[:, half:]], axis=0)


def per_device(
    residual,
    lengths,
    token_adapter_index,
    attention_norm_gain,
    query_key_weight,
    value_weight,
    head_second_weight,
    output_weight,
    adapter_down_maps,
    adapter_up_maps,
    feedforward_norm_gain,
    gate_weight,
    up_weight,
    down_weight,
):
    tokens, width = residual.shape
    groups = lax.axis_size("head")
    own_width = width // groups
    own_begin = lax.axis_index("head") * own_width
    units = gate_weight.shape[1]

    down_map = fold_map(adapter_down_maps[0].T)
    up_map = fold_map(lax.dynamic_slice_in_dim(adapter_up_maps[0], own_begin, own_width, 1))

    early = jnp.concatenate([query_key_weight, value_weight, output_weight, down_map, up_map], axis=1)
    room = jnp.zeros((gate_weight.shape[0], -units % HD), gate_weight.dtype)
    acts_own = jnp.concatenate([gate_weight, up_weight, down_weight, room], axis=1)
    acts_pair = lax.ppermute(acts_own, "head", [(i, i ^ 1) for i in range(groups)])
    early, acts_pair = lax.optimization_barrier((early, acts_pair))
    late = lax.all_gather(jnp.stack([acts_own, acts_pair]), BLK, axis=0, tiled=False)
    mine = spread(spread(early, "z"), "x")
    other = sibling(mine)
    core = lax.axis_index("core").astype(jnp.int32).reshape(1)
    sent = attention(
        lengths,
        head_second_weight,
        core,
        residual,
        attention_norm_gain,
        token_adapter_index,
        mine,
        other,
    )

    own_residual = lax.dynamic_slice_in_dim(residual, own_begin, own_width, 1)
    own_mid, halves = middle(
        core, token_adapter_index, own_residual, exchange(sent, "head"), mine, other
    )
    mid_full = exchange(halves, "head")
    piece = feed_forward(mid_full, feedforward_norm_gain, late, units)
    pieces = exchange(piece, "head").reshape(groups // 2, tokens, own_width)
    return (own_mid + jnp.sum(pieces.astype(jnp.float32), axis=0)).astype(jnp.bfloat16)


def solution(mesh):
    fine = Mesh(mesh.devices.reshape(mesh.devices.shape[0], 8, 4, 2), ("head", *BLK))
    return jax.shard_map(
        per_device,
        mesh=fine,
        in_specs=(
            P(BLK, None),
            P(BLK, None),
            P(BLK, None),
            P(),
            P(BLK, "head"),
            P(BLK, "head"),
            P("head"),
            P(BLK, "head"),
            P(BLK, "head", None),
            P(BLK, None, None),
            P(),
            P(BLK, "head"),
            P(BLK, "head"),
            P(BLK, "head"),
        ),
        out_specs=P(BLK, "head"),
        check_vma=False,
    )
```

```python
import jax
import jax.numpy as jnp
from jax import lax
from jax.experimental import pallas as pl
from jax.experimental.pallas import tpu as pltpu
from jax.sharding import Mesh
from jax.sharding import PartitionSpec as P

HD = 128
RANK = 16

adapter_scaling = 2.0
head_shrink = 0.8
neg_large = -1e30

BLK = ("z", "x", "core")


def rms_scale(values, epsilon):
    return values * lax.rsqrt(jnp.mean(values * values, axis=-1, keepdims=True) + epsilon)


def nt_dot(left, right, precision=None):
    return lax.dot_general(
        left,
        right,
        (((1,), (1,)), ((), ())),
        precision=precision,
        preferred_element_type=jnp.float32,
    )


def masked_softmax(scores, allowed):
    scores = jnp.where(allowed, scores, neg_large)
    row_peak = jnp.max(scores, axis=-1, keepdims=True)
    raised = jnp.where(allowed, jnp.exp(scores - row_peak), 0.0)
    return raised / jnp.sum(raised, axis=-1, keepdims=True)


def rank_lift(adapters):
    shape = (RANK, adapters * RANK)
    rank = lax.broadcasted_iota(jnp.int32, shape, 1) % RANK
    return jnp.where(rank == lax.broadcasted_iota(jnp.int32, shape, 0), 1.0, 0.0).astype(
        jnp.bfloat16
    )


def attention_kernel(
    lengths_ref, lambda_ref, place_ref, residual_ref, gain_ref, chosen_ref, mine_ref, other_ref, sent_ref
):
    slabs_x, slabs_z, rows, _ = mine_ref.shape
    tokens = residual_ref.shape[0]
    value_width = 2 * HD
    qkv_width = 4 * HD + value_width
    out_end = qkv_width + value_width
    adapters = 2 * slabs_x * slabs_z

    def body(even_ref, odd_ref):
        def gather(z, begin, end, first_row=0, last_row=rows):
            return jnp.concatenate(
                [
                    ref[x, z, first_row:last_row, begin:end]
                    for x in range(slabs_x)
                    for ref in (even_ref, odd_ref)
                ],
                axis=0,
            )

        slab = 2 * slabs_x * rows
        normed = (rms_scale(residual_ref[...].astype(jnp.float32), 1e-06) * gain_ref[...]).astype(
            jnp.bfloat16
        )
        qkv = jnp.zeros((tokens, qkv_width), jnp.float32)
        for z in range(slabs_z):
            qkv = qkv + jnp.dot(
                normed[:, z * slab : (z + 1) * slab],
                gather(z, 0, qkv_width),
                preferred_element_type=jnp.float32,
            )
        row_at = lax.broadcasted_iota(jnp.int32, (tokens, tokens), 0)
        column_at = lax.broadcasted_iota(jnp.int32, (tokens, tokens), 1)
        row_request = jnp.zeros((tokens, tokens), jnp.int32)
        column_request = jnp.zeros((tokens, tokens), jnp.int32)
        end = jnp.int32(0)
        for i in range(lengths_ref.shape[1]):
            end = end + lengths_ref[0, i]
            row_request = row_request + jnp.where(row_at >= end, 1, 0)
            column_request = column_request + jnp.where(column_at >= end, 1, 0)
        allowed = (row_request == column_request) & (column_at <= row_at)
        parts = [qkv[:, i * HD : (i + 1) * HD] for i in range(4)]
        scale = 1.0 / HD**0.5
        probs = [
            masked_softmax(nt_dot(parts[i], parts[i + 2], lax.Precision.HIGHEST) * scale, allowed)
            for i in range(2)
        ]
        mixed = (probs[0] - lambda_ref[0] * probs[1]).astype(jnp.bfloat16)
        attended = jnp.dot(
            mixed, qkv[:, 4 * HD :].astype(jnp.bfloat16), preferred_element_type=jnp.float32
        )
        head_out = (rms_scale(attended, 1e-05) * head_shrink).astype(jnp.bfloat16)

        room = jnp.zeros((value_width - tokens, value_width), jnp.bfloat16)
        padded = jnp.concatenate([head_out, room], axis=0)
        coordinates = jnp.zeros((adapters * RANK, value_width), jnp.float32)
        for half in range(2):
            maps = jnp.concatenate(
                [
                    gather(z, out_end, out_end + HD, half * RANK, (half + 1) * RANK)
                    for z in range(slabs_z)
                ],
                axis=0,
            )
            coordinates = coordinates + nt_dot(maps, padded[:, half * HD : (half + 1) * HD])
        owner = lax.broadcasted_iota(jnp.int32, coordinates.shape, 0) // RANK
        kept = jnp.where(owner == chosen_ref[...], coordinates, 0.0)
        high = kept.astype(jnp.bfloat16)
        low = (kept - high.astype(jnp.float32)).astype(jnp.bfloat16)
        lift = rank_lift(adapters)
        low_rows = jnp.concatenate(
            [
                jnp.dot(lift, high, preferred_element_type=jnp.float32),
                jnp.dot(lift, low, preferred_element_type=jnp.float32),
            ],
            axis=0,
        ).astype(jnp.bfloat16)
        for z in range(slabs_z):
            sent_ref[z, :tokens, :] = nt_dot(head_out, gather(z, qkv_width, out_end)).astype(
                jnp.bfloat16
            )
            sent_ref[z, tokens:, :] = low_rows

    @pl.when(place_ref[0] == 0)
    def _():
        body(mine_ref, other_ref)

    @pl.when(place_ref[0] != 0)
    def _():
        body(other_ref, mine_ref)


def attention(lengths, second_weight, place, residual, gain, chosen, mine, other):
    tokens = residual.shape[0]
    groups = mine.shape[1]
    smem = pl.BlockSpec(memory_space=pltpu.SMEM)
    vmem = pl.BlockSpec(memory_space=pltpu.VMEM)
    return pl.pallas_call(
        attention_kernel,
        out_shape=jax.ShapeDtypeStruct((groups, tokens + 2 * RANK, 2 * HD), jnp.bfloat16),
        in_specs=[smem] * 3 + [vmem] * 5,
        out_specs=vmem,
        compiler_params=pltpu.CompilerParams(vmem_limit_bytes=48 * 1024 * 1024),
        cost_estimate=pl.CostEstimate(
            flops=1_200_000_000, bytes_accessed=8_000_000, transcendentals=80_000
        ),
    )(lengths, second_weight, place, residual, gain.reshape(1, -1), chosen, mine, other)


def middle_kernel(place_ref, chosen_ref, residual_ref, received_ref, mine_ref, other_ref, mid_ref, sent_ref):
    slabs_x, slabs_z, _, half_width = mine_ref.shape
    tokens = residual_ref.shape[0]
    part = tokens // 2
    adapters = 2 * slabs_x * slabs_z

    def body(even_ref, odd_ref):
        total = received_ref[0].astype(jnp.float32)
        for group in range(1, received_ref.shape[0]):
            total = total + received_ref[group].astype(jnp.float32)
        low_rank = (total[tokens : tokens + RANK] + total[tokens + RANK :]).astype(jnp.bfloat16)
        lifted = lax.dot_general(
            rank_lift(adapters),
            low_rank,
            (((0,), (0,)), ((), ())),
            preferred_element_type=jnp.float32,
        )
        owner = lax.broadcasted_iota(jnp.int32, lifted.shape, 0) // RANK
        routed = jnp.where(owner == chosen_ref[...], lifted, 0.0).astype(jnp.bfloat16)
        for half in range(2):
            maps = jnp.concatenate(
                [
                    ref[x, z, half * RANK : (half + 1) * RANK, :]
                    for z in range(slabs_z)
                    for x in range(slabs_x)
                    for ref in (even_ref, odd_ref)
                ],
                axis=0,
            )
            product = lax.dot_general(
                routed, maps, (((0,), (0,)), ((), ())), preferred_element_type=jnp.float32
            )
            delta = (adapter_scaling * product[:tokens]).astype(jnp.bfloat16)
            lanes = slice(half * half_width, (half + 1) * half_width)
            mid = residual_ref[:, lanes].astype(jnp.float32) + total[:tokens, lanes]
            mid_ref[:, lanes] = mid + delta.astype(jnp.float32)
        rounded = mid_ref[...].astype(jnp.bfloat16)
        for group in range(sent_ref.shape[0]):
            side = group % 2
            sent_ref[group] = rounded[side * part : (side + 1) * part]

    @pl.when(place_ref[0] == 0)
    def _():
        body(mine_ref, other_ref)

    @pl.when(place_ref[0] != 0)
    def _():
        body(other_ref, mine_ref)


def middle(place, chosen, residual, received, mine, other):
    tokens = residual.shape[0]
    groups, _, own_width = received.shape
    last = mine.shape[3] // HD - 1
    maps = pl.BlockSpec((*mine.shape[:3], HD), lambda i, place_ref: (0, 0, 0, last))

    def whole(shape):
        return pl.BlockSpec(shape, lambda i, place_ref: (0,) * len(shape))

    mid_shape = (tokens, own_width)
    sent_shape = (groups, tokens // 2, own_width)
    return pl.pallas_call(
        middle_kernel,
        grid_spec=pltpu.PrefetchScalarGridSpec(
            num_scalar_prefetch=1,
            grid=(1,),
            in_specs=[
                whole(chosen.shape),
                pl.BlockSpec(mid_shape, lambda i, place_ref: (0, place_ref[1])),
                whole(received.shape),
                maps,
                maps,
            ],
            out_specs=[whole(mid_shape), whole(sent_shape)],
        ),
        out_shape=[
            jax.ShapeDtypeStruct(mid_shape, jnp.float32),
            jax.ShapeDtypeStruct(sent_shape, jnp.bfloat16),
        ],
        compiler_params=pltpu.CompilerParams(vmem_limit_bytes=32 * 1024 * 1024),
        cost_estimate=pl.CostEstimate(
            flops=120_000_000, bytes_accessed=3_000_000, transcendentals=0
        ),
    )(place, chosen, residual, received, mine, other)


def feed_forward_kernel(mid_ref, gain_ref, weights_ref, out_ref, acts_ref, down_ref, acts_in, down_in):
    sides, steps, owners, rows, pairs = acts_ref.shape
    padded = down_ref.shape[4]
    groups, _, slab = mid_ref.shape
    units = pairs // 2
    per_step = owners * rows // slab

    def fetch(side, step, begin, count, held_ref, arrived):
        return pltpu.make_async_copy(
            weights_ref.at[pl.ds(step * owners, owners), side, :, pl.ds(begin, count)],
            held_ref.at[side, step],
            arrived.at[side, step],
        )

    acts_copies = [
        [fetch(side, step, 0, pairs, acts_ref, acts_in) for step in range(steps)]
        for side in range(sides)
    ]
    down_copies = [
        [fetch(side, step, pairs, padded, down_ref, down_in) for side in range(sides)]
        for step in range(steps)
    ]
    for row in acts_copies + down_copies:
        for copy in row:
            copy.start()
    mid = mid_ref[...].astype(jnp.float32)
    square = jnp.sum(jnp.sum(mid * mid, axis=0), axis=-1, keepdims=True) / (groups * slab)
    normed = (mid * lax.rsqrt(square + 1e-06)[None] * gain_ref[...]).astype(jnp.bfloat16)

    hidden = []
    for side in range(sides):
        acts = None
        for step in range(steps):
            left = jnp.concatenate(
                [normed[step * per_step + i] for i in range(per_step)], axis=1
            )
            acts_copies[side][step].wait()
            product = jnp.dot(
                left,
                acts_ref[side, step].reshape(owners * rows, pairs),
                preferred_element_type=jnp.float32,
            )
            acts = product if acts is None else acts + product
        upward = pltpu.roll(acts, units, 1)[:, :padded]
        lane = lax.broadcasted_iota(jnp.int32, upward.shape, 1)
        gated = jax.nn.silu(acts[:, :padded]) * upward
        hidden.append(jnp.where(lane < units, gated, 0.0).astype(jnp.bfloat16))
    for step in range(steps):
        for copy in down_copies[step]:
            copy.wait()
        for i in range(per_step):
            picked = slice(i * slab, (i + 1) * slab)
            out_ref[step * per_step + i] = sum(
                nt_dot(
                    hidden[side], down_ref[side, step].reshape(owners * rows, padded)[picked]
                )
                for side in range(sides)
            ).astype(jnp.bfloat16)


def feed_forward(mid, gain, weights, units):
    groups, _, slab = mid.shape
    owners, sides, rows, columns = weights.shape
    steps = 4
    held = (sides, steps, owners // steps, rows)
    vmem = pl.BlockSpec(memory_space=pltpu.VMEM)
    return pl.pallas_call(
        feed_forward_kernel,
        out_shape=jax.ShapeDtypeStruct(mid.shape, jnp.bfloat16),
        in_specs=[vmem, vmem, pl.BlockSpec(memory_space=pl.ANY)],
        out_specs=vmem,
        scratch_shapes=[
            pltpu.VMEM((*held, 2 * units), jnp.bfloat16),
            pltpu.VMEM((*held, columns - 2 * units), jnp.bfloat16),
            pltpu.SemaphoreType.DMA((sides, steps)),
            pltpu.SemaphoreType.DMA((sides, steps)),
        ],
        compiler_params=pltpu.CompilerParams(vmem_limit_bytes=40 * 1024 * 1024),
        cost_estimate=pl.CostEstimate(
            flops=1_700_000_000, bytes_accessed=18_000_000, transcendentals=300_000
        ),
    )(mid, gain.reshape(groups, 1, slab), weights)


def exchange(blocks, axis):
    return lax.all_to_all(blocks, axis, split_axis=0, concat_axis=0, tiled=True)


def spread(block, axis):
    return exchange(jnp.broadcast_to(block[None], (lax.axis_size(axis), *block.shape)), axis)


def sibling(block):
    return lax.ppermute(block, "core", [(0, 1), (1, 0)])


def fold_map(rank_rows):
    half = rank_rows.shape[1] // 2
    return jnp.concatenate([rank_rows[:, :half], rank_rows[:, half:]], axis=0)


def per_device(
    residual,
    lengths,
    token_adapter_index,
    attention_norm_gain,
    query_key_weight,
    value_weight,
    head_second_weight,
    output_weight,
    adapter_down_maps,
    adapter_up_maps,
    feedforward_norm_gain,
    gate_weight,
    up_weight,
    down_weight,
):
    tokens, width = residual.shape
    groups = lax.axis_size("head")
    own_width = width // groups
    own_begin = lax.axis_index("head") * own_width
    units = gate_weight.shape[1]

    down_map = fold_map(adapter_down_maps[0].T)
    up_map = fold_map(lax.dynamic_slice_in_dim(adapter_up_maps[0], own_begin, own_width, 1))

    early = jnp.concatenate([query_key_weight, value_weight, output_weight, down_map, up_map], axis=1)
    room = jnp.zeros((gate_weight.shape[0], -units % HD), gate_weight.dtype)
    acts_own = jnp.concatenate([gate_weight, up_weight, down_weight, room], axis=1)
    acts_pair = lax.ppermute(acts_own, "head", [(i, i ^ 1) for i in range(groups)])
    early, acts_pair = lax.optimization_barrier((early, acts_pair))
    late = lax.all_gather(jnp.stack([acts_own, acts_pair]), BLK, axis=0, tiled=False)
    mine = spread(spread(early, "z"), "x")
    other = sibling(mine)
    place = jnp.stack([lax.axis_index("core"), lax.axis_index("head")]).astype(jnp.int32)
    chosen = jnp.pad(
        token_adapter_index.reshape(1, tokens), ((0, 0), (0, own_width - tokens)), constant_values=-1
    )
    sent = attention(
        lengths, head_second_weight, place, residual, attention_norm_gain, chosen, mine, other
    )
    own_mid, halves = middle(place, chosen, residual, exchange(sent, "head"), mine, other)
    mid_full = exchange(halves, "head")
    piece = feed_forward(mid_full, feedforward_norm_gain, late, units)
    pieces = exchange(piece, "head").reshape(groups // 2, tokens, own_width)
    return (own_mid + jnp.sum(pieces.astype(jnp.float32), axis=0)).astype(jnp.bfloat16)


def solution(mesh):
    fine = Mesh(mesh.devices.reshape(mesh.devices.shape[0], 8, 4, 2), ("head", *BLK))
    return jax.shard_map(
        per_device,
        mesh=fine,
        in_specs=(
            P(BLK, None),
            P(BLK, None),
            P(BLK, None),
            P(),
            P(BLK, "head"),
            P(BLK, "head"),
            P("head"),
            P(BLK, "head"),
            P(BLK, "head", None),
            P(BLK, None, None),
            P(),
            P(BLK, "head"),
            P(BLK, "head"),
            P(BLK, "head"),
        ),
        out_specs=P(BLK, "head"),
        check_vma=False,
    )
```

```python
import jax
import jax.numpy as jnp
from jax import lax
from jax.experimental import pallas as pl
from jax.experimental.pallas import tpu as pltpu
from jax.sharding import Mesh
from jax.sharding import PartitionSpec as P

HD = 128
RANK = 16

adapter_scaling = 2.0
head_shrink = 0.8
neg_large = -1e30

BLK = ("z", "x", "core")


def rms_scale(values, epsilon):
    return values * lax.rsqrt(jnp.mean(values * values, axis=-1, keepdims=True) + epsilon)


def nt_dot(left, right, precision=None):
    return lax.dot_general(
        left,
        right,
        (((1,), (1,)), ((), ())),
        precision=precision,
        preferred_element_type=jnp.float32,
    )


def masked_softmax(scores, allowed):
    scores = jnp.where(allowed, scores, neg_large)
    row_peak = jnp.max(scores, axis=-1, keepdims=True)
    raised = jnp.where(allowed, jnp.exp(scores - row_peak), 0.0)
    return raised / jnp.sum(raised, axis=-1, keepdims=True)


def rank_lift(adapters):
    shape = (RANK, adapters * RANK)
    rank = lax.broadcasted_iota(jnp.int32, shape, 1) % RANK
    return jnp.where(rank == lax.broadcasted_iota(jnp.int32, shape, 0), 1.0, 0.0).astype(
        jnp.bfloat16
    )


def attention_kernel(
    lengths_ref,
    lambda_ref,
    place_ref,
    residual_ref,
    gain_ref,
    chosen_ref,
    mine_ref,
    sibling_ref,
    sent_ref,
    other_ref,
    arrived,
):
    slabs_x, slabs_z, rows, _ = mine_ref.shape
    tokens = residual_ref.shape[0]
    value_width = 2 * HD
    qkv_width = 4 * HD + value_width
    out_end = qkv_width + value_width
    adapters = 2 * slabs_x * slabs_z
    copies = [
        pltpu.make_async_copy(sibling_ref.at[x], other_ref.at[x], arrived.at[x])
        for x in range(slabs_x)
    ]
    for copy in copies:
        copy.start()
    normed = (rms_scale(residual_ref[...].astype(jnp.float32), 1e-06) * gain_ref[...]).astype(
        jnp.bfloat16
    )
    for copy in copies:
        copy.wait()

    def body(even_ref, odd_ref):
        def gather(z, begin, end, first_row=0, last_row=rows):
            return jnp.concatenate(
                [
                    ref[x, z, first_row:last_row, begin:end]
                    for x in range(slabs_x)
                    for ref in (even_ref, odd_ref)
                ],
                axis=0,
            )

        slab = 2 * slabs_x * rows
        qkv = jnp.zeros((tokens, qkv_width), jnp.float32)
        for z in range(slabs_z):
            qkv = qkv + jnp.dot(
                normed[:, z * slab : (z + 1) * slab],
                gather(z, 0, qkv_width),
                preferred_element_type=jnp.float32,
            )
        row_at = lax.broadcasted_iota(jnp.int32, (tokens, tokens), 0)
        column_at = lax.broadcasted_iota(jnp.int32, (tokens, tokens), 1)
        row_request = jnp.zeros((tokens, tokens), jnp.int32)
        column_request = jnp.zeros((tokens, tokens), jnp.int32)
        end = jnp.int32(0)
        for i in range(lengths_ref.shape[1]):
            end = end + lengths_ref[0, i]
            row_request = row_request + jnp.where(row_at >= end, 1, 0)
            column_request = column_request + jnp.where(column_at >= end, 1, 0)
        allowed = (row_request == column_request) & (column_at <= row_at)
        parts = [qkv[:, i * HD : (i + 1) * HD] for i in range(4)]
        scale = 1.0 / HD**0.5
        probs = [
            masked_softmax(nt_dot(parts[i], parts[i + 2], lax.Precision.HIGHEST) * scale, allowed)
            for i in range(2)
        ]
        mixed = (probs[0] - lambda_ref[0] * probs[1]).astype(jnp.bfloat16)
        attended = jnp.dot(
            mixed, qkv[:, 4 * HD :].astype(jnp.bfloat16), preferred_element_type=jnp.float32
        )
        head_out = (rms_scale(attended, 1e-05) * head_shrink).astype(jnp.bfloat16)

        room = jnp.zeros((value_width - tokens, value_width), jnp.bfloat16)
        padded = jnp.concatenate([head_out, room], axis=0)
        coordinates = jnp.zeros((adapters * RANK, value_width), jnp.float32)
        for half in range(2):
            maps = jnp.concatenate(
                [
                    gather(z, out_end, out_end + HD, half * RANK, (half + 1) * RANK)
                    for z in range(slabs_z)
                ],
                axis=0,
            )
            coordinates = coordinates + nt_dot(maps, padded[:, half * HD : (half + 1) * HD])
        owner = lax.broadcasted_iota(jnp.int32, coordinates.shape, 0) // RANK
        kept = jnp.where(owner == chosen_ref[...], coordinates, 0.0)
        low_rows = jnp.dot(
            rank_lift(adapters), kept.astype(jnp.bfloat16), preferred_element_type=jnp.float32
        ).astype(jnp.bfloat16)
        for z in range(slabs_z):
            sent_ref[z, :tokens, :] = nt_dot(head_out, gather(z, qkv_width, out_end)).astype(
                jnp.bfloat16
            )
            sent_ref[z, tokens:, :] = low_rows

    @pl.when(place_ref[0] == 0)
    def _():
        body(mine_ref, other_ref)

    @pl.when(place_ref[0] != 0)
    def _():
        body(other_ref, mine_ref)


def attention(lengths, second_weight, place, residual, gain, chosen, mine, other):
    tokens = residual.shape[0]
    groups = mine.shape[1]
    smem = pl.BlockSpec(memory_space=pltpu.SMEM)
    vmem = pl.BlockSpec(memory_space=pltpu.VMEM)
    return pl.pallas_call(
        attention_kernel,
        out_shape=jax.ShapeDtypeStruct((groups, tokens + RANK, 2 * HD), jnp.bfloat16),
        in_specs=[smem] * 3 + [vmem] * 4 + [pl.BlockSpec(memory_space=pl.ANY)],
        out_specs=vmem,
        scratch_shapes=[
            pltpu.VMEM(other.shape, other.dtype),
            pltpu.SemaphoreType.DMA((mine.shape[0],)),
        ],
        compiler_params=pltpu.CompilerParams(vmem_limit_bytes=48 * 1024 * 1024),
        cost_estimate=pl.CostEstimate(
            flops=1_200_000_000, bytes_accessed=8_000_000, transcendentals=80_000
        ),
    )(lengths, second_weight, place, residual, gain.reshape(1, -1), chosen, mine, other)


def middle_kernel(place_ref, chosen_ref, residual_ref, received_ref, mine_ref, other_ref, mid_ref, sent_ref):
    slabs_x, slabs_z, _, half_width = mine_ref.shape
    tokens = residual_ref.shape[0]
    part = tokens // 2
    adapters = 2 * slabs_x * slabs_z

    def body(even_ref, odd_ref):
        total = received_ref[0].astype(jnp.float32)
        for group in range(1, received_ref.shape[0]):
            total = total + received_ref[group].astype(jnp.float32)
        low_rank = total[tokens:].astype(jnp.bfloat16)
        lifted = lax.dot_general(
            rank_lift(adapters),
            low_rank,
            (((0,), (0,)), ((), ())),
            preferred_element_type=jnp.float32,
        )
        owner = lax.broadcasted_iota(jnp.int32, lifted.shape, 0) // RANK
        routed = jnp.where(owner == chosen_ref[...], lifted, 0.0).astype(jnp.bfloat16)
        for half in range(2):
            maps = jnp.concatenate(
                [
                    ref[x, z, half * RANK : (half + 1) * RANK, :]
                    for z in range(slabs_z)
                    for x in range(slabs_x)
                    for ref in (even_ref, odd_ref)
                ],
                axis=0,
            )
            product = lax.dot_general(
                routed, maps, (((0,), (0,)), ((), ())), preferred_element_type=jnp.float32
            )
            delta = (adapter_scaling * product[:tokens]).astype(jnp.bfloat16)
            lanes = slice(half * half_width, (half + 1) * half_width)
            mid = residual_ref[:, lanes].astype(jnp.float32) + total[:tokens, lanes]
            mid_ref[:, lanes] = mid + delta.astype(jnp.float32)
        rounded = mid_ref[...].astype(jnp.bfloat16)
        for group in range(sent_ref.shape[0]):
            side = group % 2
            sent_ref[group] = rounded[side * part : (side + 1) * part]

    @pl.when(place_ref[0] == 0)
    def _():
        body(mine_ref, other_ref)

    @pl.when(place_ref[0] != 0)
    def _():
        body(other_ref, mine_ref)


def middle(place, chosen, residual, received, mine, other):
    tokens = residual.shape[0]
    groups, _, own_width = received.shape
    last = mine.shape[3] // HD - 1
    maps = pl.BlockSpec((*mine.shape[:3], HD), lambda i, place_ref: (0, 0, 0, last))

    def whole(shape):
        return pl.BlockSpec(shape, lambda i, place_ref: (0,) * len(shape))

    mid_shape = (tokens, own_width)
    sent_shape = (groups, tokens // 2, own_width)
    return pl.pallas_call(
        middle_kernel,
        grid_spec=pltpu.PrefetchScalarGridSpec(
            num_scalar_prefetch=1,
            grid=(1,),
            in_specs=[
                whole(chosen.shape),
                pl.BlockSpec(mid_shape, lambda i, place_ref: (0, place_ref[1])),
                whole(received.shape),
                maps,
                maps,
            ],
            out_specs=[whole(mid_shape), whole(sent_shape)],
        ),
        out_shape=[
            jax.ShapeDtypeStruct(mid_shape, jnp.float32),
            jax.ShapeDtypeStruct(sent_shape, jnp.bfloat16),
        ],
        compiler_params=pltpu.CompilerParams(vmem_limit_bytes=32 * 1024 * 1024),
        cost_estimate=pl.CostEstimate(
            flops=120_000_000, bytes_accessed=3_000_000, transcendentals=0
        ),
    )(place, chosen, residual, received, mine, other)


def feed_forward_kernel(mid_ref, gain_ref, weights_ref, out_ref, acts_ref, down_ref, acts_in, down_in):
    sides, steps, owners, rows, pairs = acts_ref.shape
    padded = down_ref.shape[4]
    groups, _, slab = mid_ref.shape
    units = pairs // 2
    per_step = owners * rows // slab

    def fetch(side, step, begin, count, held_ref, arrived):
        return pltpu.make_async_copy(
            weights_ref.at[pl.ds(step * owners, owners), side, :, pl.ds(begin, count)],
            held_ref.at[side, step],
            arrived.at[side, step],
        )

    acts_copies = [
        [fetch(side, step, 0, pairs, acts_ref, acts_in) for step in range(steps)]
        for side in range(sides)
    ]
    down_copies = [
        [fetch(side, step, pairs, padded, down_ref, down_in) for side in range(sides)]
        for step in range(steps)
    ]
    for row in acts_copies + down_copies:
        for copy in row:
            copy.start()
    mid = mid_ref[...].astype(jnp.float32)
    square = jnp.sum(jnp.sum(mid * mid, axis=0), axis=-1, keepdims=True) / (groups * slab)
    normed = (mid * lax.rsqrt(square + 1e-06)[None] * gain_ref[...]).astype(jnp.bfloat16)

    hidden = []
    for side in range(sides):
        acts = None
        for step in range(steps):
            left = jnp.concatenate(
                [normed[step * per_step + i] for i in range(per_step)], axis=1
            )
            acts_copies[side][step].wait()
            product = jnp.dot(
                left,
                acts_ref[side, step].reshape(owners * rows, pairs),
                preferred_element_type=jnp.float32,
            )
            acts = product if acts is None else acts + product
        upward = pltpu.roll(acts, units, 1)[:, :padded]
        lane = lax.broadcasted_iota(jnp.int32, upward.shape, 1)
        gated = jax.nn.silu(acts[:, :padded]) * upward
        hidden.append(jnp.where(lane < units, gated, 0.0).astype(jnp.bfloat16))
    for step in range(steps):
        for copy in down_copies[step]:
            copy.wait()
        for i in range(per_step):
            picked = slice(i * slab, (i + 1) * slab)
            out_ref[step * per_step + i] = sum(
                nt_dot(
                    hidden[side], down_ref[side, step].reshape(owners * rows, padded)[picked]
                )
                for side in range(sides)
            ).astype(jnp.bfloat16)


def feed_forward(mid, gain, weights, units):
    groups, _, slab = mid.shape
    owners, sides, rows, columns = weights.shape
    steps = 4
    held = (sides, steps, owners // steps, rows)
    vmem = pl.BlockSpec(memory_space=pltpu.VMEM)
    return pl.pallas_call(
        feed_forward_kernel,
        out_shape=jax.ShapeDtypeStruct(mid.shape, jnp.bfloat16),
        in_specs=[vmem, vmem, pl.BlockSpec(memory_space=pl.ANY)],
        out_specs=vmem,
        scratch_shapes=[
            pltpu.VMEM((*held, 2 * units), jnp.bfloat16),
            pltpu.VMEM((*held, columns - 2 * units), jnp.bfloat16),
            pltpu.SemaphoreType.DMA((sides, steps)),
            pltpu.SemaphoreType.DMA((sides, steps)),
        ],
        compiler_params=pltpu.CompilerParams(vmem_limit_bytes=40 * 1024 * 1024),
        cost_estimate=pl.CostEstimate(
            flops=1_700_000_000, bytes_accessed=18_000_000, transcendentals=300_000
        ),
    )(mid, gain.reshape(groups, 1, slab), weights)


def exchange(blocks, axis):
    return lax.all_to_all(blocks, axis, split_axis=0, concat_axis=0, tiled=True)


def spread(block, axis):
    return exchange(jnp.broadcast_to(block[None], (lax.axis_size(axis), *block.shape)), axis)


def sibling(block):
    return lax.ppermute(block, "core", [(0, 1), (1, 0)])


def fold_map(rank_rows):
    half = rank_rows.shape[1] // 2
    return jnp.concatenate([rank_rows[:, :half], rank_rows[:, half:]], axis=0)


def per_device(
    residual,
    lengths,
    token_adapter_index,
    attention_norm_gain,
    query_key_weight,
    value_weight,
    head_second_weight,
    output_weight,
    adapter_down_maps,
    adapter_up_maps,
    feedforward_norm_gain,
    gate_weight,
    up_weight,
    down_weight,
):
    tokens, width = residual.shape
    groups = lax.axis_size("head")
    own_width = width // groups
    own_begin = lax.axis_index("head") * own_width
    units = gate_weight.shape[1]

    down_map = fold_map(adapter_down_maps[0].T)
    up_map = fold_map(lax.dynamic_slice_in_dim(adapter_up_maps[0], own_begin, own_width, 1))

    early = jnp.concatenate([query_key_weight, value_weight, output_weight, down_map, up_map], axis=1)
    room = jnp.zeros((gate_weight.shape[0], -units % HD), gate_weight.dtype)
    acts_own = jnp.concatenate([gate_weight, up_weight, down_weight, room], axis=1)
    acts_pair = lax.ppermute(acts_own, "head", [(i, i ^ 1) for i in range(groups)])
    early, acts_pair = lax.optimization_barrier((early, acts_pair))
    late = lax.all_gather(jnp.stack([acts_own, acts_pair]), BLK, axis=0, tiled=False)
    mine = spread(spread(early, "z"), "x")
    other = sibling(mine)
    place = jnp.stack([lax.axis_index("core"), lax.axis_index("head")]).astype(jnp.int32)
    chosen = jnp.pad(
        token_adapter_index.reshape(1, tokens), ((0, 0), (0, own_width - tokens)), constant_values=-1
    )
    sent = attention(
        lengths, head_second_weight, place, residual, attention_norm_gain, chosen, mine, other
    )
    own_mid, halves = middle(place, chosen, residual, exchange(sent, "head"), mine, other)
    mid_full = exchange(halves, "head")
    piece = feed_forward(mid_full, feedforward_norm_gain, late, units)
    pieces = exchange(piece, "head").reshape(groups // 2, tokens, own_width)
    return (own_mid + jnp.sum(pieces.astype(jnp.float32), axis=0)).astype(jnp.bfloat16)


def solution(mesh):
    fine = Mesh(mesh.devices.reshape(mesh.devices.shape[0], 8, 4, 2), ("head", *BLK))
    return jax.shard_map(
        per_device,
        mesh=fine,
        in_specs=(
            P(BLK, None),
            P(BLK, None),
            P(BLK, None),
            P(),
            P(BLK, "head"),
            P(BLK, "head"),
            P("head"),
            P(BLK, "head"),
            P(BLK, "head", None),
            P(BLK, None, None),
            P(),
            P(BLK, "head"),
            P(BLK, "head"),
            P(BLK, "head"),
        ),
        out_specs=P(BLK, "head"),
        check_vma=False,
    )
```

```python
import jax
import jax.numpy as jnp
from jax import lax
from jax.experimental import pallas as pl
from jax.experimental.pallas import tpu as pltpu
from jax.sharding import Mesh
from jax.sharding import PartitionSpec as P

HD = 128
RANK = 16

adapter_scaling = 2.0
head_shrink = 0.8
neg_large = -1e30

BLK = ("z", "x", "core")


def rms_scale(values, epsilon):
    return values * lax.rsqrt(jnp.mean(values * values, axis=-1, keepdims=True) + epsilon)


def nt_dot(left, right, precision=None):
    return lax.dot_general(
        left,
        right,
        (((1,), (1,)), ((), ())),
        precision=precision,
        preferred_element_type=jnp.float32,
    )


def masked_softmax(scores, allowed):
    scores = jnp.where(allowed, scores, neg_large)
    row_peak = jnp.max(scores, axis=-1, keepdims=True)
    raised = jnp.where(allowed, jnp.exp(scores - row_peak), 0.0)
    return raised / jnp.sum(raised, axis=-1, keepdims=True)


def rank_lift(adapters):
    shape = (RANK, adapters * RANK)
    rank = lax.broadcasted_iota(jnp.int32, shape, 1) % RANK
    return jnp.where(rank == lax.broadcasted_iota(jnp.int32, shape, 0), 1.0, 0.0).astype(
        jnp.bfloat16
    )


def attention_kernel(
    lengths_ref,
    lambda_ref,
    place_ref,
    residual_ref,
    gain_ref,
    chosen_ref,
    mine_ref,
    other_ref,
    sent_ref,
):
    slabs_x, slabs_z, rows, _ = mine_ref.shape
    tokens = residual_ref.shape[0]
    value_width = 2 * HD
    qkv_width = 4 * HD + value_width
    out_end = qkv_width + value_width
    adapters = 2 * slabs_x * slabs_z
    normed = (rms_scale(residual_ref[...].astype(jnp.float32), 1e-06) * gain_ref[...]).astype(
        jnp.bfloat16
    )

    def body(even_ref, odd_ref):
        def gather(z, begin, end, first_row=0, last_row=rows):
            return jnp.concatenate(
                [
                    ref[x, z, first_row:last_row, begin:end]
                    for x in range(slabs_x)
                    for ref in (even_ref, odd_ref)
                ],
                axis=0,
            )

        slab = 2 * slabs_x * rows
        depth = slabs_z // 2
        qkv = sum(
            jnp.dot(
                normed[:, z * slab : (z + depth) * slab],
                jnp.concatenate([gather(z + i, 0, qkv_width) for i in range(depth)], axis=0),
                preferred_element_type=jnp.float32,
            )
            for z in range(0, slabs_z, depth)
        )
        row_at = lax.broadcasted_iota(jnp.int32, (tokens, tokens), 0)
        column_at = lax.broadcasted_iota(jnp.int32, (tokens, tokens), 1)
        row_request = jnp.zeros((tokens, tokens), jnp.int32)
        column_request = jnp.zeros((tokens, tokens), jnp.int32)
        end = jnp.int32(0)
        for i in range(lengths_ref.shape[1]):
            end = end + lengths_ref[0, i]
            row_request = row_request + jnp.where(row_at >= end, 1, 0)
            column_request = column_request + jnp.where(column_at >= end, 1, 0)
        allowed = (row_request == column_request) & (column_at <= row_at)
        parts = [qkv[:, i * HD : (i + 1) * HD] for i in range(4)]
        scale = 1.0 / HD**0.5
        probs = [
            masked_softmax(nt_dot(parts[i], parts[i + 2], lax.Precision.HIGHEST) * scale, allowed)
            for i in range(2)
        ]
        mixed = (probs[0] - lambda_ref[0] * probs[1]).astype(jnp.bfloat16)
        attended = jnp.dot(
            mixed, qkv[:, 4 * HD :].astype(jnp.bfloat16), preferred_element_type=jnp.float32
        )
        head_out = (rms_scale(attended, 1e-05) * head_shrink).astype(jnp.bfloat16)

        room = jnp.zeros((value_width - tokens, value_width), jnp.bfloat16)
        padded = jnp.concatenate([head_out, room], axis=0)
        coordinates = jnp.zeros((adapters * RANK, value_width), jnp.float32)
        for half in range(2):
            maps = jnp.concatenate(
                [
                    gather(z, out_end, out_end + HD, half * RANK, (half + 1) * RANK)
                    for z in range(slabs_z)
                ],
                axis=0,
            )
            coordinates = coordinates + nt_dot(maps, padded[:, half * HD : (half + 1) * HD])
        owner = lax.broadcasted_iota(jnp.int32, coordinates.shape, 0) // RANK
        kept = jnp.where(owner == chosen_ref[...], coordinates, 0.0)
        low_rows = jnp.dot(
            rank_lift(adapters), kept.astype(jnp.bfloat16), preferred_element_type=jnp.float32
        ).astype(jnp.bfloat16)
        for z in range(slabs_z):
            sent_ref[z, :tokens, :] = nt_dot(head_out, gather(z, qkv_width, out_end)).astype(
                jnp.bfloat16
            )
            sent_ref[z, tokens:, :] = low_rows

    @pl.when(place_ref[0] == 0)
    def _():
        body(mine_ref, other_ref)

    @pl.when(place_ref[0] != 0)
    def _():
        body(other_ref, mine_ref)


def attention(lengths, second_weight, place, residual, gain, chosen, mine, other):
    tokens = residual.shape[0]
    groups = mine.shape[1]
    smem = pl.BlockSpec(memory_space=pltpu.SMEM)
    vmem = pl.BlockSpec(memory_space=pltpu.VMEM)
    return pl.pallas_call(
        attention_kernel,
        out_shape=jax.ShapeDtypeStruct((groups, tokens + RANK, 2 * HD), jnp.bfloat16),
        in_specs=[smem] * 3 + [vmem] * 5,
        out_specs=vmem,
        compiler_params=pltpu.CompilerParams(vmem_limit_bytes=48 * 1024 * 1024),
        cost_estimate=pl.CostEstimate(
            flops=1_200_000_000, bytes_accessed=8_000_000, transcendentals=80_000
        ),
    )(lengths, second_weight, place, residual, gain.reshape(1, -1), chosen, mine, other)


def middle_kernel(place_ref, chosen_ref, residual_ref, received_ref, mine_ref, other_ref, mid_ref, sent_ref):
    slabs_x, slabs_z, _, half_width = mine_ref.shape
    tokens = residual_ref.shape[0]
    part = tokens // 2
    adapters = 2 * slabs_x * slabs_z

    def body(even_ref, odd_ref):
        total = received_ref[0].astype(jnp.float32)
        for group in range(1, received_ref.shape[0]):
            total = total + received_ref[group].astype(jnp.float32)
        low_rank = total[tokens:].astype(jnp.bfloat16)
        lifted = lax.dot_general(
            rank_lift(adapters),
            low_rank,
            (((0,), (0,)), ((), ())),
            preferred_element_type=jnp.float32,
        )
        owner = lax.broadcasted_iota(jnp.int32, lifted.shape, 0) // RANK
        routed = jnp.where(owner == chosen_ref[...], lifted, 0.0).astype(jnp.bfloat16)
        for half in range(2):
            maps = jnp.concatenate(
                [
                    ref[x, z, half * RANK : (half + 1) * RANK, :]
                    for z in range(slabs_z)
                    for x in range(slabs_x)
                    for ref in (even_ref, odd_ref)
                ],
                axis=0,
            )
            product = lax.dot_general(
                routed, maps, (((0,), (0,)), ((), ())), preferred_element_type=jnp.float32
            )
            delta = (adapter_scaling * product[:tokens]).astype(jnp.bfloat16)
            lanes = slice(half * half_width, (half + 1) * half_width)
            mid = residual_ref[:, lanes].astype(jnp.float32) + total[:tokens, lanes]
            mid_ref[:, lanes] = mid + delta.astype(jnp.float32)
        rounded = mid_ref[...].astype(jnp.bfloat16)
        for group in range(sent_ref.shape[0]):
            side = group % 2
            sent_ref[group] = rounded[side * part : (side + 1) * part]

    @pl.when(place_ref[0] == 0)
    def _():
        body(mine_ref, other_ref)

    @pl.when(place_ref[0] != 0)
    def _():
        body(other_ref, mine_ref)


def middle(place, chosen, residual, received, mine, other):
    tokens = residual.shape[0]
    groups, _, own_width = received.shape
    last = mine.shape[3] // HD - 1
    maps = pl.BlockSpec((*mine.shape[:3], HD), lambda i, place_ref: (0, 0, 0, last))

    def whole(shape):
        return pl.BlockSpec(shape, lambda i, place_ref: (0,) * len(shape))

    mid_shape = (tokens, own_width)
    sent_shape = (groups, tokens // 2, own_width)
    return pl.pallas_call(
        middle_kernel,
        grid_spec=pltpu.PrefetchScalarGridSpec(
            num_scalar_prefetch=1,
            grid=(1,),
            in_specs=[
                whole(chosen.shape),
                pl.BlockSpec(mid_shape, lambda i, place_ref: (0, place_ref[1])),
                whole(received.shape),
                maps,
                maps,
            ],
            out_specs=[whole(mid_shape), whole(sent_shape)],
        ),
        out_shape=[
            jax.ShapeDtypeStruct(mid_shape, jnp.float32),
            jax.ShapeDtypeStruct(sent_shape, jnp.bfloat16),
        ],
        compiler_params=pltpu.CompilerParams(vmem_limit_bytes=32 * 1024 * 1024),
        cost_estimate=pl.CostEstimate(
            flops=120_000_000, bytes_accessed=3_000_000, transcendentals=0
        ),
    )(place, chosen, residual, received, mine, other)


def feed_forward_kernel(mid_ref, gain_ref, weights_ref, out_ref, acts_ref, down_ref, acts_in, down_in):
    sides, steps, owners, rows, pairs = acts_ref.shape
    padded = down_ref.shape[4]
    groups, _, slab = mid_ref.shape
    units = pairs // 2
    per_step = owners * rows // slab

    def fetch(side, step, begin, count, held_ref, arrived):
        return pltpu.make_async_copy(
            weights_ref.at[pl.ds(step * owners, owners), side, :, pl.ds(begin, count)],
            held_ref.at[side, step],
            arrived.at[side, step],
        )

    acts_copies = [
        [fetch(side, step, 0, pairs, acts_ref, acts_in) for step in range(steps)]
        for side in range(sides)
    ]
    down_copies = [
        [fetch(side, step, pairs, padded, down_ref, down_in) for side in range(sides)]
        for step in range(steps)
    ]
    for row in acts_copies + down_copies:
        for copy in row:
            copy.start()
    mid = mid_ref[...].astype(jnp.float32)
    square = jnp.sum(jnp.sum(mid * mid, axis=0), axis=-1, keepdims=True) / (groups * slab)
    normed = (mid * lax.rsqrt(square + 1e-06)[None] * gain_ref[...]).astype(jnp.bfloat16)

    hidden = []
    for side in range(sides):
        acts = None
        for step in range(steps):
            left = jnp.concatenate(
                [normed[step * per_step + i] for i in range(per_step)], axis=1
            )
            acts_copies[side][step].wait()
            product = jnp.dot(
                left,
                acts_ref[side, step].reshape(owners * rows, pairs),
                preferred_element_type=jnp.float32,
            )
            acts = product if acts is None else acts + product
        upward = pltpu.roll(acts, units, 1)[:, :padded]
        lane = lax.broadcasted_iota(jnp.int32, upward.shape, 1)
        gated = jax.nn.silu(acts[:, :padded]) * upward
        hidden.append(jnp.where(lane < units, gated, 0.0).astype(jnp.bfloat16))
    for step in range(steps):
        for copy in down_copies[step]:
            copy.wait()
        for i in range(per_step):
            picked = slice(i * slab, (i + 1) * slab)
            out_ref[step * per_step + i] = sum(
                nt_dot(
                    hidden[side], down_ref[side, step].reshape(owners * rows, padded)[picked]
                )
                for side in range(sides)
            ).astype(jnp.bfloat16)


def feed_forward(mid, gain, weights, units):
    groups, _, slab = mid.shape
    owners, sides, rows, columns = weights.shape
    steps = 4
    held = (sides, steps, owners // steps, rows)
    vmem = pl.BlockSpec(memory_space=pltpu.VMEM)
    return pl.pallas_call(
        feed_forward_kernel,
        out_shape=jax.ShapeDtypeStruct(mid.shape, jnp.bfloat16),
        in_specs=[vmem, vmem, pl.BlockSpec(memory_space=pl.ANY)],
        out_specs=vmem,
        scratch_shapes=[
            pltpu.VMEM((*held, 2 * units), jnp.bfloat16),
            pltpu.VMEM((*held, columns - 2 * units), jnp.bfloat16),
            pltpu.SemaphoreType.DMA((sides, steps)),
            pltpu.SemaphoreType.DMA((sides, steps)),
        ],
        compiler_params=pltpu.CompilerParams(vmem_limit_bytes=40 * 1024 * 1024),
        cost_estimate=pl.CostEstimate(
            flops=1_700_000_000, bytes_accessed=18_000_000, transcendentals=300_000
        ),
    )(mid, gain.reshape(groups, 1, slab), weights)


def exchange(blocks, axis):
    return lax.all_to_all(blocks, axis, split_axis=0, concat_axis=0, tiled=True)


def spread(block, axis):
    return exchange(jnp.broadcast_to(block[None], (lax.axis_size(axis), *block.shape)), axis)


def sibling(block):
    return lax.ppermute(block, "core", [(0, 1), (1, 0)])


def fold_map(rank_rows):
    half = rank_rows.shape[1] // 2
    return jnp.concatenate([rank_rows[:, :half], rank_rows[:, half:]], axis=0)


def per_device(
    residual,
    lengths,
    token_adapter_index,
    attention_norm_gain,
    query_key_weight,
    value_weight,
    head_second_weight,
    output_weight,
    adapter_down_maps,
    adapter_up_maps,
    feedforward_norm_gain,
    gate_weight,
    up_weight,
    down_weight,
):
    tokens, width = residual.shape
    groups = lax.axis_size("head")
    own_width = width // groups
    own_begin = lax.axis_index("head") * own_width
    units = gate_weight.shape[1]

    down_map = fold_map(adapter_down_maps[0].T)
    up_map = fold_map(lax.dynamic_slice_in_dim(adapter_up_maps[0], own_begin, own_width, 1))

    early = jnp.concatenate([query_key_weight, value_weight, output_weight, down_map, up_map], axis=1)
    room = jnp.zeros((gate_weight.shape[0], -units % HD), gate_weight.dtype)
    acts_own = jnp.concatenate([gate_weight, up_weight, down_weight, room], axis=1)
    acts_pair = lax.ppermute(acts_own, "head", [(i, i ^ 1) for i in range(groups)])
    early, acts_pair = lax.optimization_barrier((early, acts_pair))
    late = lax.all_gather(jnp.stack([acts_own, acts_pair]), BLK, axis=0, tiled=False)
    mine = spread(spread(early, "z"), "x")
    other = sibling(mine)
    place = jnp.stack([lax.axis_index("core"), lax.axis_index("head")]).astype(jnp.int32)
    chosen = jnp.pad(
        token_adapter_index.reshape(1, tokens), ((0, 0), (0, own_width - tokens)), constant_values=-1
    )
    sent = attention(
        lengths, head_second_weight, place, residual, attention_norm_gain, chosen, mine, other
    )
    own_mid, halves = middle(place, chosen, residual, exchange(sent, "head"), mine, other)
    mid_full = exchange(halves, "head")
    piece = feed_forward(mid_full, feedforward_norm_gain, late, units)
    pieces = exchange(piece, "head").reshape(groups // 2, tokens, own_width)
    return (own_mid + jnp.sum(pieces.astype(jnp.float32), axis=0)).astype(jnp.bfloat16)


def solution(mesh):
    fine = Mesh(mesh.devices.reshape(mesh.devices.shape[0], 8, 4, 2), ("head", *BLK))
    return jax.shard_map(
        per_device,
        mesh=fine,
        in_specs=(
            P(BLK, None),
            P(BLK, None),
            P(BLK, None),
            P(),
            P(BLK, "head"),
            P(BLK, "head"),
            P("head"),
            P(BLK, "head"),
            P(BLK, "head", None),
            P(BLK, None, None),
            P(),
            P(BLK, "head"),
            P(BLK, "head"),
            P(BLK, "head"),
        ),
        out_specs=P(BLK, "head"),
        check_vma=False,
    )
```
